32 devices in a mesh: req: 8 (over z, y), grp: 4 (over x, core).
Axes of the slice: x: 2, y: 2, z: 4, core: 2. Of those that a mesh axis runs over, the one named last changes fastest.
Arguments:
- suffix_queries: bfloat16 [4, 1024, 1024], P('grp', 'req'), may hold values from -140 to 140
- suffix_keys: bfloat16 [4, 1024, 1024], P('grp', 'req'), may hold values from -6 to 6
- suffix_values: bfloat16 [4, 1024, 1024], P('grp', 'req'), may hold values from -6 to 6
- prefix_cache: bfloat16 [4, 32, 2048], P('grp', 'req'), may hold values from -6 to 6
- residual: bfloat16 [4, 1024, 2048], P('grp', 'req'), may hold values from -6 to 6
- out_weight: bfloat16 [1024, 2048], P(('req', 'grp')), may hold values from -0.1875 to 0.1875
- norm_gain: float32 [2048], replicated, may hold values from 0.5 to 1.5
- routes: int32 [4, 1024, 4], P('grp', 'req'), may hold values from 0 to 7, all different within a row; in each aligned block of 128 rows (0 to 127, 128 to 255, ..., all dimensions but the last counted through in order) at most 80 rows name the same one
- route_weights: float32 [4, 1024, 4], P('grp', 'req'), may hold values from 0.05 to 0.6
- lengths: int32 [4, 16], P('grp'), may hold values from 1 to 256, 1024 in all within a row
- migrate: int32 [2, 64], P(None, 'req'), may hold values 0 or 1
- expert_gate: bfloat16 [8, 2048, 704], P('req', None, 'grp'), may hold values from -0.125 to 0.125
- expert_up: bfloat16 [8, 2048, 704], P('req', None, 'grp'), may hold values from -0.125 to 0.125
- expert_down: bfloat16 [8, 704, 2048], P('req', 'grp'), may hold values from -0.21875 to 0.21875
- shared_gate: bfloat16 [2048, 2816], P(None, 'grp'), may hold values from -0.125 to 0.125
- shared_up: bfloat16 [2048, 2816], P(None, 'grp'), may hold values from -0.125 to 0.125
- shared_down: bfloat16 [2816, 2048], P('grp'), may hold values from -0.109375 to 0.109375
- shared_router: bfloat16 [2048], replicated, may hold values from -0.125 to 0.125
Outputs:
- hidden_out: bfloat16 [4, 1024, 2048], P('grp', 'req')
- suffix_cache: bfloat16 [4, 1024, 2048], P('grp', 'req')
The draws below stay inside these ranges and needn't reach their ends.
Inputs may be any that keep to these rules, and one draw needn't show every extreme that they name: In each aligned block of 128 tokens no expert is named by more than 80 routes, a bound that some block reaches. Each group's lengths sum to 1024; the longest is exactly 256.
All inputs are finite; a program needn't handle non-finite values. No bound on the sum of `migrate` on one device may be relied on, other than what follows from the above.
Results may differ from the reference program's by a relative error of at most 0.0069.
Values may be sent and summed in bfloat16 or wider, within the bound.
No kernel may reach another device: no remote copies, remote signals or barrier semaphores. Data moves between devices by JAX's collectives and lax.ppermute only.
A program may use at most 128 MiB of HBM per device.

```python
import math
import jax
import jax.numpy as jnp
import numpy as np
from jax import lax

D = 2048
HD = 128
HEADS = 8
EFF = 704
SH = 2816
TOP = 4
PG = 16
REQS = 16
TOK_DEV = 128
EXPERTS = 8
CAP = 80
TOKENS_G = 1024
PREFIX = 32
MAXLEN = 256
HIST = 2
GROUPS = 4
PAGES = 64


def joint_draw(key):
    base = jax.random.fold_in(key, 17)
    key_first, key_second = jax.random.split(base, 2)
    shape = (GROUPS, TOKENS_G, HEADS * HD)
    key_field = jnp.clip(jax.random.normal(key_first, shape, jnp.float32), -6.0, 6.0)
    query_field = jnp.clip(4.0 * jax.random.normal(key_second, shape, jnp.float32), -24.0, 24.0)
    return (query_field, key_field)


def draw_suffix_queries(key, part):
    return joint_draw(key)[0].astype(jnp.bfloat16)


def draw_suffix_keys(key, part):
    return joint_draw(key)[1].astype(jnp.bfloat16)


def with_ends(array, own_key, low, largest):
    shape = array.shape
    spot = [jax.random.randint(jax.random.fold_in(own_key, axis), (), 0, shape[axis]) for axis in range(len(shape))]
    array = array.at[tuple(spot)].set(low)
    longest = shape.index(max(shape))
    spot[longest] = (spot[longest] + 1) % shape[longest]
    return array.at[tuple(spot)].set(largest)


def block_scale(own_key, dims, cuts, smallest, high):
    loudness = 1.0
    for dim, shards_of in cuts:
        steps = jax.random.uniform(jax.random.fold_in(jax.random.fold_in(own_key, 6), dim), (shards_of,), jnp.float32, smallest / len(cuts), high / len(cuts))
        loudness = loudness * jnp.repeat(jnp.exp(steps), dims[dim] // shards_of).reshape((-1,) + (1,) * (len(dims) - 1 - dim))
    return loudness


def length_profile(count, total, bound, skew):
    loads = [(1 << 20) // math.isqrt(grade ** skew) + 1 for grade in range(2, count + 1)]
    spare, counts = total - bound - (count - 1), [1] * (count - 1)
    while spare > 0:
        movable = [i for i in range(count - 1) if counts[i] < bound]
        pool, left = sum([loads[i] for i in movable]), spare
        for i in movable:
            more = min(bound - counts[i], max(1, left * loads[i] // pool), spare)
            counts[i] = counts[i] + more
            spare = spare - more
    return np.array([bound] + counts)


def ragged_sizes(key, number_of, total, bound, lean):
    if number_of == 2:
        one = jax.random.randint(key, (), max(1, total - bound), min(bound, total - 1) + 1)
        return jnp.stack([one, total - one])
    sizes = jnp.asarray(length_profile(number_of, total, bound, lean), jnp.int32)
    couples = (number_of - 1) // 2
    donor, receiver = sizes[1:1 + 2 * couples:2], sizes[2:2 + 2 * couples:2]
    margin = jnp.minimum(donor - 1, bound - receiver)
    passed = jax.random.randint(jax.random.fold_in(key, 1), (couples,), 0, 1 << 20) % (margin + 1)
    sizes = sizes.at[1:1 + 2 * couples:2].set(donor - passed).at[2:2 + 2 * couples:2].set(receiver + passed)
    return sizes[jax.random.permutation(jax.random.fold_in(key, 2), number_of)]


def assign_block(own_key, own, number, rows, number_of, top, limit, lean):
    ranking = jax.random.permutation(own_key, number_of)
    crowded, usual = load_shares(number_of, rows * top, limit, lean, True), load_shares(number_of, rows * top, limit, lean, False)
    places = jnp.arange(number_of)

    def named(sizes, offset_by):
        used = int((sizes > 0).sum())
        fixed = max(1, used // 4)
        shifted = fixed + (places - fixed + offset_by * (used - fixed)) % max(1, number_of - fixed)
        return jnp.zeros((number_of,), jnp.int32).at[ranking[jnp.where(places < fixed, places, shifted)]].set(jnp.asarray(sizes, jnp.int32))

    sizes = jnp.where(number % 4 == 0, named(crowded, number // 4), named(usual, number - number // 4 - 1))
    mixed = jax.random.permutation(jax.random.fold_in(own, 3), number_of)
    source_of, sink = mixed[0:number_of // 2 * 2:2], mixed[1:number_of // 2 * 2:2]
    slack = jnp.minimum(sizes[source_of] - 1, limit - sizes[sink]) // 2
    slack = jnp.where((source_of == ranking[0]) | (sink == ranking[0]) | (sizes[sink] == 0), 0, jnp.maximum(slack, 0))
    shifted = jax.random.randint(jax.random.fold_in(own, 4), (number_of // 2,), 0, 1 << 20) % (slack + 1)
    sizes = sizes.at[source_of].add(-shifted).at[sink].add(shifted)
    items = jnp.searchsorted(jnp.cumsum(sizes), jnp.arange(rows * top), side="right").astype(jnp.int32)
    listing = items.reshape(top, rows).T
    listing = listing[jax.random.permutation(jax.random.fold_in(own, 1), rows)]
    offset_by = jax.random.randint(jax.random.fold_in(own, 2), (rows, 1), 0, top)
    return jnp.take_along_axis(listing, (jnp.arange(top)[None, :] + offset_by) % top, axis=1)


def load_shares(amount, total, reach, lean, full):
    portions = [(1 << 20) // math.isqrt(grade ** lean) + 1 for grade in range(1, amount + 1)]
    largest = reach if full else min(reach, max(-(-total // amount), total * portions[0] // sum(portions)))
    least = 1 if total - largest >= amount - 1 else 0
    holding, rest = [largest] + [least] * (amount - 1), total - largest - least * (amount - 1)
    while rest > 0:
        free = [i for i in range(1, amount) if holding[i] < largest] or [i for i in range(1, amount) if holding[i] < reach]
        pool, left = sum([portions[i] for i in free]), rest
        for i in free:
            extra = min(reach - holding[i], max(1, left * portions[i] // pool), rest)
            holding[i] = holding[i] + extra
            rest = rest - extra
    return np.array(holding)


def bell_draw(stream_key, extent, spread, bound, cuts=(), kind=jnp.bfloat16):
    level = block_scale(stream_key, extent, cuts, -0.22, 0.18) if cuts else 1.0
    values = jax.random.normal(stream_key, extent, jnp.float32) * spread * level
    return jnp.minimum(jnp.maximum(values, -bound), bound).astype(kind)


def setup_inputs(seed: int = 0) -> dict:
    streams_of = jax.random.split(jax.random.key(seed), 19)
    suffix_queries = draw_suffix_queries(jax.random.fold_in(streams_of[18], 71), 0)
    suffix_keys = draw_suffix_keys(jax.random.fold_in(streams_of[18], 71), 0)
    suffix_values = bell_draw(streams_of[2], (GROUPS, TOKENS_G, HEADS * HD), 1.0, 6.0, ((0, 4), (1, 8)))
    prefix_cache = bell_draw(streams_of[3], (GROUPS, PREFIX, 2 * HEADS * HD), 1.0, 6.0, ((0, 4), (1, 8)))
    residual = bell_draw(streams_of[4], (GROUPS, TOKENS_G, D), 1.0, 6.0, ((0, 4), (1, 8)))
    out_weight = bell_draw(streams_of[5], (HEADS * HD, D), (HEADS * HD) ** -0.5, 0.1875, ((0, 32),))
    norm_gain = jnp.clip(1.0 + 0.1 * jax.random.normal(streams_of[6], (D,), jnp.float32), 0.5, 1.5)
    routes_keys = jax.random.split(jax.random.fold_in(streams_of[7], 1), GROUPS * TOKENS_G // TOK_DEV)
    routes_turns = jax.random.permutation(jax.random.fold_in(streams_of[7], 3), GROUPS * TOKENS_G // TOK_DEV)
    routes = jax.vmap(lambda own, number: assign_block(jax.random.fold_in(streams_of[7], 2), own, number, TOK_DEV, EXPERTS, TOP, CAP, 2))(routes_keys, routes_turns).reshape((GROUPS, TOKENS_G, TOP))
    route_weights = jnp.clip(jnp.exp(math.log(0.6) - 2.4849067 * jax.random.uniform(streams_of[8], (GROUPS, TOKENS_G, TOP), jnp.float32) ** block_scale(streams_of[8], (GROUPS, TOKENS_G, TOP), ((0, 4), (1, 8)), -0.2, 0.2)), 0.05, 0.6)
    lengths = jax.vmap(lambda own: ragged_sizes(own, REQS, TOKENS_G, MAXLEN, 2))(jax.random.split(streams_of[9], GROUPS)).reshape((GROUPS, REQS)).astype(jnp.int32)
    migrate = with_ends((jax.random.randint(streams_of[10], (GROUPS // 2, PAGES), 0, 2) < 1).astype(jnp.int32), jax.random.fold_in(streams_of[10], 1), 0, 1)
    expert_gate = bell_draw(streams_of[11], (EXPERTS, D, EFF), D ** -0.5, 0.125, ((0, 8), (2, 4)))
    expert_up = bell_draw(streams_of[12], (EXPERTS, D, EFF), D ** -0.5, 0.125, ((0, 8), (2, 4)))
    expert_down = bell_draw(streams_of[13], (EXPERTS, EFF, D), EFF ** -0.5, 0.21875, ((0, 8), (1, 4)))
    shared_gate = bell_draw(streams_of[14], (D, SH), D ** -0.5, 0.125, ((1, 4),))
    shared_up = bell_draw(streams_of[15], (D, SH), D ** -0.5, 0.125, ((1, 4),))
    shared_down = bell_draw(streams_of[16], (SH, D), SH ** -0.5, 0.109375, ((0, 4),))
    shared_router = bell_draw(streams_of[17], (D,), D ** -0.5, 0.125)
    return {"suffix_queries": suffix_queries, "suffix_keys": suffix_keys, "suffix_values": suffix_values, "prefix_cache": prefix_cache, "residual": residual, "out_weight": out_weight, "norm_gain": norm_gain, "routes": routes, "route_weights": route_weights, "lengths": lengths, "migrate": migrate, "expert_gate": expert_gate, "expert_up": expert_up, "expert_down": expert_down, "shared_gate": shared_gate, "shared_up": shared_up, "shared_down": shared_down, "shared_router": shared_router}


ROPE_BASE = 1000000.0
EPSILON = 1e-06

def request_index(token_ids, length_row):
    request_ends = jnp.cumsum(length_row).astype(jnp.int32)
    starts = (request_ends - length_row).astype(jnp.int32)
    request = lax.optimization_barrier(jnp.sum((token_ids[:, None] >= request_ends[None, :]).astype(jnp.int32), axis=1)).astype(jnp.int32)
    onehot = request[:, None] == jnp.arange(length_row.shape[0], dtype=jnp.int32)[None, :]
    opening = lax.optimization_barrier(jnp.sum(jnp.where(onehot, starts[None, :], 0), axis=1)).astype(jnp.int32)
    return (request, (token_ids - opening).astype(jnp.int32))

def rope_rows(entries, positions):
    half_size = HD // 2
    indices = jnp.arange(half_size, dtype=jnp.float32)
    inv_freq = jnp.power(ROPE_BASE, -2.0 * indices / HD)
    angles = positions[:, None] * inv_freq[None, :]
    cosine = jnp.cos(angles)[:, None, :]
    sine_part = jnp.sin(angles)[:, None, :]
    per_head = entries.astype(jnp.float32).reshape(entries.shape[0], HEADS, HD)
    first_half = per_head[..., :half_size]
    second = per_head[..., half_size:]
    turned = jnp.concatenate([first_half * cosine - second * sine_part, second * cosine + first_half * sine_part], axis=-1)
    return turned.reshape(entries.shape[0], HEADS * HD).astype(jnp.bfloat16)

def attend(query_block, key_rows, value_rows, allowed):
    count_rows = query_block.shape[0]
    query_heads = query_block.astype(jnp.float32).reshape(count_rows, HEADS, HD)
    key_heads = key_rows.astype(jnp.float32).reshape(key_rows.shape[0], HEADS, HD)
    value_heads = value_rows.astype(jnp.float32).reshape(value_rows.shape[0], HEADS, HD)
    scores = jnp.einsum('qhd,khd->hqk', query_heads, key_heads) * HD ** (-0.5)
    scores = jnp.where(allowed[None], scores, -1e+30)
    highest = lax.optimization_barrier(jnp.max(scores, axis=2, keepdims=True))
    weights = jnp.where(allowed[None], jnp.exp(scores - highest), 0.0)
    totals = lax.optimization_barrier(jnp.sum(weights, axis=2, keepdims=True))
    probabilities = weights.astype(jnp.bfloat16).astype(jnp.float32)
    blended = jnp.einsum('hqk,khd->hqd', probabilities, value_heads) / totals
    return jnp.transpose(blended, (1, 0, 2)).reshape(count_rows, HEADS * HD).astype(jnp.bfloat16)

def expert_outputs(matrix_rows, gate_matrix, up_matrix, down_matrix):
    gate_part = jnp.dot(matrix_rows, gate_matrix, preferred_element_type=jnp.float32)
    up_part = jnp.dot(matrix_rows, up_matrix, preferred_element_type=jnp.float32)
    hidden = (jax.nn.silu(gate_part) * up_part).astype(jnp.bfloat16)
    return jnp.dot(hidden, down_matrix, preferred_element_type=jnp.float32).astype(jnp.bfloat16)

def reference(suffix_queries, suffix_keys, suffix_values, prefix_cache, residual, out_weight, norm_gain, routes, route_weights, lengths, migrate, expert_gate, expert_up, expert_down, shared_gate, shared_up, shared_down, shared_router):
    width_all = HEADS * HD
    span = HIST * TOK_DEV
    attention_groups = []
    cache_groups = []
    for group in range(GROUPS):
        length_row = lengths[group]
        token_ids = jnp.arange(TOKENS_G, dtype=jnp.int32)
        offset = request_index(token_ids, length_row)[1]
        positions = (PREFIX + offset).astype(jnp.float32)
        query_turned = rope_rows(suffix_queries[group], positions)
        key_turned = rope_rows(suffix_keys[group], positions)
        cache_groups.append(jnp.concatenate([key_turned, suffix_values[group]], axis=1))
        padded_keys = jnp.concatenate([jnp.zeros((span, width_all), jnp.bfloat16), key_turned], axis=0)
        padded_values = jnp.concatenate([jnp.zeros((span, width_all), jnp.bfloat16), suffix_values[group]], axis=0)
        prefix_keys = prefix_cache[group, :, :width_all]
        prefix_values = prefix_cache[group, :, width_all:]

        def one_block(block, length_row=length_row, query_turned=query_turned, padded_keys=padded_keys, padded_values=padded_values, prefix_keys=prefix_keys, prefix_values=prefix_values):
            first_row = (block * TOK_DEV).astype(jnp.int32)
            query_block = lax.dynamic_slice_in_dim(query_turned, first_row, TOK_DEV, 0)
            key_block = lax.dynamic_slice_in_dim(padded_keys, first_row, span + TOK_DEV, 0)
            value_block = lax.dynamic_slice_in_dim(padded_values, first_row, span + TOK_DEV, 0)
            query_ids = (first_row + jnp.arange(TOK_DEV, dtype=jnp.int32)).astype(jnp.int32)
            key_ids = (first_row - span + jnp.arange(span + TOK_DEV, dtype=jnp.int32)).astype(jnp.int32)
            query_request = request_index(query_ids, length_row)[0]
            key_request = request_index(jnp.maximum(key_ids, 0), length_row)[0]
            allowed = (key_ids[None, :] >= 0) & (key_request[None, :] == query_request[:, None]) & (key_ids[None, :] <= query_ids[:, None])
            allowed = jnp.concatenate([jnp.ones((TOK_DEV, PREFIX), jnp.bool_), allowed], axis=1)
            key_rows = jnp.concatenate([prefix_keys, key_block], axis=0)
            value_rows = jnp.concatenate([prefix_values, value_block], axis=0)
            return attend(query_block, key_rows, value_rows, allowed)
        outcome = lax.map(one_block, jnp.arange(TOKENS_G // TOK_DEV, dtype=jnp.int32))
        attention_groups.append(outcome.reshape(TOKENS_G, width_all))
    attention = jnp.concatenate(attention_groups, axis=0)
    state = residual.reshape(-1, D).astype(jnp.float32) + jnp.dot(attention, out_weight, preferred_element_type=jnp.float32)
    normed = (state * lax.rsqrt(lax.optimization_barrier(jnp.mean(state * state, axis=1, keepdims=True)) + EPSILON) * norm_gain).astype(jnp.bfloat16)
    quarter = SH // GROUPS
    shared_out = jnp.zeros(state.shape, jnp.float32)
    for block in range(GROUPS):
        gate_part = jnp.dot(normed, shared_gate[:, block * quarter:(block + 1) * quarter], preferred_element_type=jnp.float32)
        up_part = jnp.dot(normed, shared_up[:, block * quarter:(block + 1) * quarter], preferred_element_type=jnp.float32)
        hidden = (jax.nn.silu(gate_part) * up_part).astype(jnp.bfloat16)
        partial_sum = jnp.dot(hidden, shared_down[block * quarter:(block + 1) * quarter], preferred_element_type=jnp.float32).astype(jnp.bfloat16)
        partial_sum = lax.optimization_barrier(partial_sum)
        shared_out = shared_out + partial_sum.astype(jnp.float32)
    shared_scale = jax.nn.sigmoid(jnp.dot(normed, shared_router, preferred_element_type=jnp.float32))
    flat_routes = routes.reshape(-1)
    flat_weights = route_weights.reshape(-1)
    owner_rows = (jnp.arange(flat_routes.shape[0], dtype=jnp.int32) // TOP).astype(jnp.int32)
    slots_total = GROUPS * (TOKENS_G // TOK_DEV) * CAP

    def add_expert(carry, member):
        number, gate_matrix, up_matrix, down_matrix = member
        struck = flat_routes == number
        order = (jnp.cumsum(struck.astype(jnp.int32)) - 1).astype(jnp.int32)
        target = jnp.where(struck, order, slots_total).astype(jnp.int32)
        token_of = jnp.zeros((slots_total,), jnp.int32).at[target].set(owner_rows, mode='drop')
        weight_of = jnp.zeros((slots_total,), jnp.float32).at[target].set(flat_weights, mode='drop')
        outputs = expert_outputs(normed[token_of], gate_matrix, up_matrix, down_matrix)
        carry = carry.at[token_of].add(weight_of[:, None] * outputs.astype(jnp.float32))
        return (carry, None)
    routed = lax.scan(add_expert, jnp.zeros(state.shape, jnp.float32), (jnp.arange(EXPERTS, dtype=jnp.int32), expert_gate, expert_up, expert_down))[0]
    final = state + shared_scale[:, None] * shared_out + routed
    hidden_out = final.astype(jnp.bfloat16).reshape(GROUPS, TOKENS_G, D)
    moved_groups = []
    for group in range(GROUPS):
        pair_row = group // 4 * 2 + group % 2
        page_moved = jnp.repeat(migrate[pair_row], PG) == 1
        moved_groups.append(jnp.where(page_moved[:, None], cache_groups[group ^ 2], cache_groups[group]))
    suffix_cache = jnp.stack(moved_groups, axis=0)
    return (hidden_out, suffix_cache)
```

```python
import functools
import math

import jax
import jax.numpy as jnp
import numpy as np
from jax import lax
from jax.experimental import pallas as pl
from jax.experimental.pallas import tpu as pltpu
from jax.sharding import PartitionSpec as P

D = 2048
HD = 128
HEADS = 8
WIDTH = HEADS * HD
TOP = 4
PG = 16
ROPE_BASE = 1000000.0
EPSILON = 1e-06
F32 = jnp.float32
BF16 = jnp.bfloat16
VMEM = pl.BlockSpec(memory_space=pltpu.VMEM)
SMEM = pl.BlockSpec(memory_space=pltpu.SMEM)
ANY = pl.BlockSpec(memory_space=pl.ANY)
NT = (((1,), (1,)), ((), ()))


def request_starts(lengths_ref, token_ids):
    start = jnp.zeros_like(token_ids)
    end = jnp.int32(0)
    for request in range(lengths_ref.shape[1]):
        end = end + lengths_ref[0, request]
        start = jnp.where(token_ids >= end, end, start)
    return start


def rope_kernel(prefix_len, lengths_ref, place_ref, inv_ref, q_ref, k_ref, v_ref, turned_ref, cache_ref):
    rows = q_ref.shape[0]
    shape = (rows, HD)
    token_ids = place_ref[0] * rows + lax.broadcasted_iota(jnp.int32, shape, 0)
    offset = token_ids - request_starts(lengths_ref, token_ids)
    angles = (prefix_len + offset).astype(F32) * inv_ref[...]
    cosine = jnp.cos(angles)
    sine = jnp.sin(angles)
    sine = jnp.where(lax.broadcasted_iota(jnp.int32, shape, 1) < HD // 2, -sine, sine)
    for head in range(HEADS):
        cols = slice(head * HD, (head + 1) * HD)
        for source, target in ((q_ref, turned_ref), (k_ref, cache_ref)):
            entries = source[:, cols].astype(F32)
            turned = entries * cosine + pltpu.roll(entries, HD // 2, 1) * sine
            target[:, cols] = turned.astype(BF16)
    cache_ref[:, WIDTH:] = v_ref[...]


def attend_kernel(depth, lengths_ref, place_ref, q_ref, prefix_ref, *refs):
    blocks, out_ref = refs[: depth + 1], refs[depth + 1]
    rows = q_ref.shape[0]
    prefix_len = prefix_ref.shape[0]
    first = place_ref[0] * rows
    ids = lax.broadcasted_iota(jnp.int32, (rows, rows), 0) + first
    start = request_starts(lengths_ref, ids)
    allowed = [jnp.ones((rows, prefix_len), jnp.bool_)]
    for distance in range(depth + 1):
        keys = lax.broadcasted_iota(jnp.int32, (rows, rows), 1) + (first - distance * rows)
        allowed.append((keys <= ids) & (keys >= start))
    bias = jnp.concatenate([jnp.where(a, 0.0, -1e30) for a in allowed], axis=1)
    keep = bias == 0.0
    sources = (prefix_ref,) + blocks
    for head in range(HEADS):
        cols = slice(head * HD, (head + 1) * HD)
        values_at = slice(WIDTH + head * HD, WIDTH + (head + 1) * HD)
        keys = jnp.concatenate([s[:, cols] for s in sources], axis=0)
        values = jnp.concatenate([s[:, values_at] for s in sources], axis=0)
        scores = lax.dot_general(q_ref[:, cols], keys, NT, preferred_element_type=F32)
        scores = jnp.where(keep, scores * HD ** (-0.5), -1e30)
        highest = jnp.max(scores, axis=1, keepdims=True)
        weights = jnp.where(keep, jnp.exp(scores - highest), 0.0)
        total = jnp.sum(weights, axis=1, keepdims=True)
        blended = jnp.dot(weights.astype(BF16), values, preferred_element_type=F32) / total
        out_ref[:, cols] = blended.astype(BF16)


def slot_experts(slots, capacity, experts, shape, dim):
    slot = lax.broadcasted_iota(jnp.int32, shape, dim).astype(F32)
    expert = jnp.floor((slot + 0.5) * (1.0 / capacity))
    return expert, slot - expert * capacity


def members(routes_ref, experts):
    rows = routes_ref.shape[0]
    numbers = lax.broadcasted_iota(jnp.int32, (rows, experts), 1)
    found = [routes_ref[:, k : k + 1] == numbers for k in range(TOP)]
    member = jnp.where(found[0] | found[1] | found[2] | found[3], 1.0, 0.0)
    above = lax.broadcasted_iota(jnp.int32, (rows, rows), 0) > lax.broadcasted_iota(
        jnp.int32, (rows, rows), 1
    )
    rank = jnp.dot(
        jnp.where(above, 1.0, 0.0).astype(BF16), member.astype(BF16), preferred_element_type=F32
    )
    return found, jnp.where(member > 0.5, rank, -1.0).astype(BF16)


def project_kernel(
    experts, capacity, moves, count, place_ref, attn_ref, residual_ref, gain_ref, router_ref, routes_ref, *refs
):
    pieces = refs[:count]
    state_ref, normed_ref, scale_ref, out_ref, weight, sem = refs[count:]
    for piece, source, rows, target in moves(place_ref):
        pltpu.make_async_copy(
            pieces[piece].at[pl.ds(source, rows)], weight.at[pl.ds(target, rows)], sem
        ).start()
    _, rank = members(routes_ref, experts)
    slots = experts * capacity
    slot_expert, slot_rank = slot_experts(slots, capacity, experts, (slots, 128), 0)
    columns = lax.broadcasted_iota(jnp.int32, (slots, experts), 1).astype(F32)
    select = jnp.where(slot_expert[:, :experts] == columns, 1.0, 0.0).astype(BF16)
    wanted = lax.dot_general(select, rank, NT, preferred_element_type=F32)
    pick = jnp.where(wanted == slot_rank, 1.0, 0.0).astype(BF16)
    pltpu.make_async_copy(weight, weight, sem).wait()
    step = 512
    square = jnp.zeros((attn_ref.shape[0], 1), F32)
    for at in range(0, D, step):
        cols = slice(at, at + step)
        part = residual_ref[:, cols].astype(F32) + jnp.dot(
            attn_ref[...], weight[:, cols], preferred_element_type=F32
        )
        state_ref[:, cols] = part
        square = square + jnp.sum(part * part, axis=1, keepdims=True)
    factor = lax.rsqrt(square * (1.0 / D) + EPSILON)
    logit = jnp.zeros_like(square)
    for at in range(0, D, step):
        cols = slice(at, at + step)
        normed = (state_ref[:, cols] * factor * gain_ref[:, cols]).astype(BF16)
        normed_ref[:, cols] = normed
        logit = logit + jnp.sum(
            normed.astype(F32) * router_ref[:, cols].astype(F32), axis=1, keepdims=True
        )
        out_ref[:, cols] = jnp.dot(pick, normed, preferred_element_type=F32).astype(BF16)
    scale_ref[...] = jnp.broadcast_to(jax.nn.sigmoid(logit), scale_ref.shape)


def ffn_kernel(xs, shards, outs, shard_rows, *refs):
    x_refs, refs = refs[:xs], refs[xs:]
    g_refs, refs = refs[:shards], refs[shards:]
    u_refs, refs = refs[:shards], refs[shards:]
    d_refs, refs = refs[:shards], refs[shards:]
    out_refs, refs = refs[:outs], refs[outs:]
    x, gate, up, down, hidden, sems = refs
    hid = shards * shard_rows
    padded = hidden.shape[1]
    waits = []
    at = 0
    for ref in x_refs:
        pltpu.make_async_copy(ref, x.at[pl.ds(at, ref.shape[0])], sems.at[0]).start()
        at += ref.shape[0]
    for target, sources, sem in ((gate, g_refs, 1), (up, u_refs, 2), (down, d_refs, 3)):
        for number, ref in enumerate(sources):
            pltpu.make_async_copy(
                ref, target.at[pl.ds(number * shard_rows, shard_rows)], sems.at[sem]
            ).start()
    if padded > hid:
        for target in (gate, up, down):
            target[hid:, :] = jnp.zeros((padded - hid, D), BF16)

    def wait(target, rows, sem):
        part = target.at[pl.ds(0, rows)]
        pltpu.make_async_copy(part, part, sems.at[sem]).wait()

    wait(x, x.shape[0], 0)
    wait(gate, hid, 1)
    wait(up, hid, 2)
    chunk = 256

    @pl.loop(0, padded // chunk)
    def _(j):
        rows = pl.ds(pl.multiple_of(j * chunk, chunk), chunk)
        g = lax.dot_general(x[...], gate[rows, :], NT, preferred_element_type=F32)
        u = lax.dot_general(x[...], up[rows, :], NT, preferred_element_type=F32)
        hidden[:, rows] = (g / (1.0 + jnp.exp(-g)) * u).astype(BF16)

    wait(down, hid, 3)

    @pl.loop(0, D // chunk)
    def _(j):
        cols = pl.ds(pl.multiple_of(j * chunk, chunk), chunk)
        result = jnp.dot(hidden[...], down[:, cols], preferred_element_type=F32).astype(BF16)
        at = 0
        for ref in out_refs:
            ref[:, cols] = result[at : at + ref.shape[0]]
            at += ref.shape[0]


def ffn(x_list, gates, ups, downs, out_rows):
    shard_rows = gates[0].shape[0]
    shards = len(gates)
    padded = -(-shards * shard_rows // 256) * 256
    rows = sum(x.shape[0] for x in x_list)
    return pl.pallas_call(
        functools.partial(ffn_kernel, len(x_list), shards, len(out_rows), shard_rows),
        out_shape=[jax.ShapeDtypeStruct((n, D), BF16) for n in out_rows],
        in_specs=[ANY] * (len(x_list) + 3 * shards),
        out_specs=[VMEM] * len(out_rows),
        scratch_shapes=[
            pltpu.VMEM((rows, D), BF16),
            pltpu.VMEM((padded, D), BF16),
            pltpu.VMEM((padded, D), BF16),
            pltpu.VMEM((padded, D), BF16),
            pltpu.VMEM((rows, padded), BF16),
            pltpu.SemaphoreType.DMA((4,)),
        ],
        compiler_params=pltpu.CompilerParams(vmem_limit_bytes=48 << 20),
        cost_estimate=pl.CostEstimate(
            flops=6 * rows * padded * D, bytes_accessed=6 * padded * D + 4 * rows * D, transcendentals=rows * padded
        ),
    )(*x_list, *gates, *ups, *downs)


def combine_kernel(
    experts, capacity, state_ref, scale_ref, routes_ref, weights_ref, back_ref, keep_ref, sib_ref, far_ref, out_ref
):
    found, rank = members(routes_ref, experts)
    slots = experts * capacity
    slot_expert, slot_rank = slot_experts(slots, capacity, experts, (experts, slots), 1)
    numbers = lax.broadcasted_iota(jnp.int32, (experts, slots), 0).astype(F32)
    select = jnp.where(slot_expert == numbers, 1.0, 0.0).astype(BF16)
    mine = jnp.dot(rank, select, preferred_element_type=F32) == slot_rank[:1]
    weight = jnp.zeros(rank.shape, F32)
    for k in range(TOP):
        weight = weight + jnp.where(found[k], weights_ref[:, k : k + 1], 0.0)
    high = weight.astype(BF16)
    low = (weight - high.astype(F32)).astype(BF16)
    spread = [
        jnp.where(mine, jnp.dot(part, select, preferred_element_type=F32), 0.0).astype(BF16)
        for part in (high, low)
    ]
    rows = state_ref.shape[0]
    scale = scale_ref[:, :1]
    step = 512
    for at in range(0, D, step):
        cols = slice(at, at + step)
        back = back_ref[:, cols]
        routed = jnp.dot(spread[0], back, preferred_element_type=F32) + jnp.dot(
            spread[1], back, preferred_element_type=F32
        )
        shared = (
            keep_ref[:rows, cols].astype(F32)
            + sib_ref[:rows, cols].astype(F32)
            + far_ref[:, cols].astype(F32)
        )
        out_ref[:, cols] = (state_ref[:, cols] + scale * shared + routed).astype(BF16)


def vmem_call(kernel, out_shape, specs, limit=32, scratch=(), flops=0):
    return pl.pallas_call(
        kernel,
        out_shape=out_shape,
        in_specs=specs,
        out_specs=jax.tree.map(lambda _: VMEM, out_shape),
        scratch_shapes=scratch,
        compiler_params=pltpu.CompilerParams(vmem_limit_bytes=limit << 20),
        cost_estimate=pl.CostEstimate(flops=flops, bytes_accessed=4 << 20, transcendentals=0),
    )


def shape(*dims, dtype=BF16):
    return jax.ShapeDtypeStruct(dims, dtype)


def grp_move(array, flip):
    return lax.ppermute(array, "grp", [(i, i ^ flip) for i in range(lax.axis_size("grp"))])


def req_shift(array, distance):
    devices = range(lax.axis_size("req"))
    return lax.ppermute(array, "req", [(i - distance, i) for i in devices if i - distance in devices])


def gather_projection(out_weight, requests):
    part = out_weight.shape[0]
    if requests != 8:
        full = lax.all_gather(out_weight, ("req", "grp"), axis=0, tiled=True)
        return [full], lambda place_ref: [(0, 0, full.shape[0], 0)]
    half = part // 2
    ring = [out_weight] + [
        lax.ppermute(out_weight, "req", [(i, (i + 2 * d) % 8) for i in range(8)]) for d in range(1, 4)
    ]

    def over_y(array):
        return lax.ppermute(array, "req", [(i, i ^ 1) for i in range(8)])

    first = jnp.concatenate([w[:half] for w in ring], axis=0)
    second = jnp.concatenate([w[half:] for w in ring], axis=0)
    first = jnp.concatenate([first, over_y(first)], axis=0)
    second = jnp.concatenate([second, grp_move(second, 2)], axis=0)
    first = jnp.concatenate([first, grp_move(first, 2)], axis=0)
    second = jnp.concatenate([second, over_y(second)], axis=0)
    pieces = [first, second, grp_move(first, 1), grp_move(second, 1)]

    def moves(place_ref):
        req, grp = place_ref[0], place_ref[1]
        listing = []
        for number in range(4):
            for outer in range(2):
                for inner in range(2):
                    for d in range(4):
                        y_flip, x_flip = (inner, outer) if number % 2 == 0 else (outer, inner)
                        row = lax.rem(req + 8 - 2 * d, 8) ^ y_flip
                        col = grp ^ (2 * x_flip + number // 2)
                        target = (row * 4 + col) * part + (number % 2) * half
                        source = ((outer * 2 + inner) * 4 + d) * half
                        listing.append((number, source, half, pl.multiple_of(target, half)))
        return listing

    return pieces, moves


def local(
    suffix_queries,
    suffix_keys,
    suffix_values,
    prefix_cache,
    residual,
    out_weight,
    norm_gain,
    routes,
    route_weights,
    lengths,
    migrate,
    expert_gate,
    expert_up,
    expert_down,
    shared_gate,
    shared_up,
    shared_down,
    shared_router,
):
    rows = suffix_queries.shape[1]
    requests = lax.axis_size("req")
    req = lax.axis_index("req")
    grp = lax.axis_index("grp")
    depth = min(8, requests // 4)
    prefix_len = prefix_cache.shape[1] * requests
    capacity = rows * TOP * 5 // (4 * requests)
    place = jnp.stack([req, grp]).astype(jnp.int32)

    inverse = ROPE_BASE ** (-2.0 * np.arange(HD // 2) / HD)
    inverse = jnp.asarray(np.concatenate([inverse, inverse])[None].astype(np.float32))
    query_turned, own_cache = vmem_call(
        functools.partial(rope_kernel, prefix_len),
        [shape(rows, WIDTH), shape(rows, 2 * WIDTH)],
        [SMEM, SMEM] + [VMEM] * 4,
    )(lengths, place, inverse, suffix_queries[0], suffix_keys[0], suffix_values[0])

    prefix_rows = lax.all_gather(prefix_cache[0], "req", axis=0, tiled=True)
    history = [req_shift(own_cache, distance) for distance in range(1, depth + 1)]
    pieces, moves = gather_projection(out_weight, requests)

    attention = vmem_call(
        functools.partial(attend_kernel, depth),
        shape(rows, WIDTH),
        [SMEM, SMEM] + [VMEM] * (3 + depth),
    )(lengths, place, query_turned, prefix_rows, own_cache, *history)

    slots = requests * capacity
    state, normed, scale, outgoing = pl.pallas_call(
        functools.partial(project_kernel, requests, capacity, moves, len(pieces)),
        out_shape=[shape(rows, D, dtype=F32), shape(rows, D), shape(rows, HD, dtype=F32), shape(slots, D)],
        in_specs=[SMEM] + [VMEM] * 5 + [ANY] * len(pieces),
        out_specs=[VMEM] * 4,
        scratch_shapes=[pltpu.VMEM((WIDTH, D), BF16), pltpu.SemaphoreType.DMA],
        compiler_params=pltpu.CompilerParams(vmem_limit_bytes=32 << 20),
        cost_estimate=pl.CostEstimate(flops=2 * rows * WIDTH * D, bytes_accessed=8 << 20, transcendentals=0),
    )(place, attention, residual[0], norm_gain[None], shared_router[None], routes[0], *pieces)

    arrived = lax.all_to_all(
        outgoing.reshape(requests, capacity, D), "req", split_axis=0, concat_axis=0, tiled=True
    ).reshape(slots, D)

    mine = [jnp.swapaxes(expert_gate[0], 0, 1), jnp.swapaxes(expert_up[0], 0, 1), expert_down[0]]
    far = [grp_move(w, 2) for w in mine]
    shards = [mine, [grp_move(w, 1) for w in mine], far, [grp_move(w, 1) for w in far]]

    far_rows = grp_move(normed, 2)
    sib_rows = grp_move(normed, 1)
    far_sib_rows = grp_move(far_rows, 1)
    keep, send = ffn(
        [normed, far_rows, sib_rows, far_sib_rows],
        [jnp.swapaxes(shared_gate, 0, 1)],
        [jnp.swapaxes(shared_up, 0, 1)],
        [shared_down],
        [2 * rows, 2 * rows],
    )
    from_sib = grp_move(send, 1)
    pair_sum = (keep[rows:].astype(F32) + from_sib[rows:].astype(F32)).astype(BF16)
    from_far = grp_move(pair_sum, 2)

    (finished,) = ffn(
        [arrived], [s[0] for s in shards], [s[1] for s in shards], [s[2] for s in shards], [slots]
    )
    back = lax.all_to_all(
        finished.reshape(requests, capacity, D), "req", split_axis=0, concat_axis=0, tiled=True
    ).reshape(slots, D)

    final = vmem_call(
        functools.partial(combine_kernel, requests, capacity), shape(rows, D), [VMEM] * 8
    )(state, scale, routes[0], route_weights[0], back, keep, from_sib, from_far)

    partner = grp_move(own_cache, 2)
    pair_row = grp // 4 * 2 + grp % 2
    flags = jnp.sum(
        jnp.where((jnp.arange(migrate.shape[0], dtype=jnp.int32) == pair_row)[:, None], migrate, 0), axis=0
    )
    page_moved = jnp.repeat(flags, PG) == 1
    suffix_cache = jnp.where(page_moved[:, None], partner, own_cache)
    return (final[None], suffix_cache[None])


def solution(mesh):
    placed = (
        P("grp", "req", None),
        P("grp", "req", None),
        P("grp", "req", None),
        P("grp", "req", None),
        P("grp", "req", None),
        P(("req", "grp"), None),
        P(),
        P("grp", "req", None),
        P("grp", "req", None),
        P("grp", None),
        P(None, "req"),
        P("req", None, "grp"),
        P("req", None, "grp"),
        P("req", "grp", None),
        P(None, "grp"),
        P(None, "grp"),
        P("grp", None),
        P(),
    )
    return jax.shard_map(
        local,
        mesh=mesh,
        in_specs=placed,
        out_specs=(P("grp", "req", None), P("grp", "req", None)),
        check_vma=False,
    )
```

```python
import functools
import math

import jax
import jax.numpy as jnp
import numpy as np
from jax import lax
from jax.experimental import pallas as pl
from jax.experimental.pallas import tpu as pltpu
from jax.sharding import PartitionSpec as P

D = 2048
HD = 128
HEADS = 8
WIDTH = HEADS * HD
TOP = 4
PG = 16
ROPE_BASE = 1000000.0
EPSILON = 1e-06
ATTEND_COST = 20_000_000_000
F32 = jnp.float32
BF16 = jnp.bfloat16
VMEM = pl.BlockSpec(memory_space=pltpu.VMEM)
SMEM = pl.BlockSpec(memory_space=pltpu.SMEM)
HBM = pl.BlockSpec(memory_space=pltpu.HBM)
ANY = pl.BlockSpec(memory_space=pl.ANY)
NT = (((1,), (1,)), ((), ()))


def request_starts(lengths_ref, token_ids):
    start = jnp.zeros_like(token_ids)
    end = jnp.int32(0)
    for request in range(lengths_ref.shape[1]):
        end = end + lengths_ref[0, request]
        start = jnp.where(token_ids >= end, end, start)
    return start


def rope_kernel(prefix_len, lengths_ref, place_ref, inv_ref, q_ref, k_ref, v_ref, turned_ref, cache_ref):
    rows = q_ref.shape[0]
    shape = (rows, HD)
    token_ids = place_ref[0] * rows + lax.broadcasted_iota(jnp.int32, shape, 0)
    offset = token_ids - request_starts(lengths_ref, token_ids)
    angles = (prefix_len + offset).astype(F32) * inv_ref[...]
    cosine = jnp.cos(angles)
    sine = jnp.sin(angles)
    sine = jnp.where(lax.broadcasted_iota(jnp.int32, shape, 1) < HD // 2, -sine, sine)
    for head in range(HEADS):
        cols = slice(head * HD, (head + 1) * HD)
        for source, target in ((q_ref, turned_ref), (k_ref, cache_ref)):
            entries = source[:, cols].astype(F32)
            turned = entries * cosine + pltpu.roll(entries, HD // 2, 1) * sine
            target[:, cols] = turned.astype(BF16)
    cache_ref[:, WIDTH:] = v_ref[...]


def attend_kernel(depth, lengths_ref, place_ref, q_ref, prefix_ref, *refs):
    blocks, order, out_ref = refs[: depth + 1], refs[depth + 1 : -1], refs[-1]
    rows = q_ref.shape[0]
    prefix_len = prefix_ref.shape[0]
    first = place_ref[0] * rows
    ids = lax.broadcasted_iota(jnp.int32, (rows, rows), 0) + first
    start = request_starts(lengths_ref, ids)
    allowed = [jnp.ones((rows, prefix_len), jnp.bool_)]
    for distance in range(depth + 1):
        keys = lax.broadcasted_iota(jnp.int32, (rows, rows), 1) + (first - distance * rows)
        allowed.append((keys <= ids) & (keys >= start))
    bias = jnp.concatenate([jnp.where(a, 0.0, -1e30) for a in allowed], axis=1)
    keep = bias == 0.0
    sources = (prefix_ref,) + blocks
    for head in range(HEADS):
        cols = slice(head * HD, (head + 1) * HD)
        values_at = slice(WIDTH + head * HD, WIDTH + (head + 1) * HD)
        keys = jnp.concatenate([s[:, cols] for s in sources], axis=0)
        values = jnp.concatenate([s[:, values_at] for s in sources], axis=0)
        scores = lax.dot_general(q_ref[:, cols], keys, NT, preferred_element_type=F32)
        scores = jnp.where(keep, scores * HD ** (-0.5), -1e30)
        highest = jnp.max(scores, axis=1, keepdims=True)
        weights = jnp.where(keep, jnp.exp(scores - highest), 0.0)
        total = jnp.sum(weights, axis=1, keepdims=True)
        blended = jnp.dot(weights.astype(BF16), values, preferred_element_type=F32) / total
        out_ref[:, cols] = blended.astype(BF16)
    if order:
        out_ref[...] = jnp.dot(out_ref[...], order[0][...], preferred_element_type=F32).astype(BF16)


def route_kernel(experts, parts, base_ref, routing_ref, pick_ref, high_ref, low_ref):
    rows = routing_ref.shape[0]
    numbers = (lax.broadcasted_iota(jnp.int32, (rows, experts), 1) + base_ref[0]).astype(F32)
    found = [routing_ref[:, k : k + 1] == numbers for k in range(TOP)]
    member = jnp.where(found[0] | found[1] | found[2] | found[3], 1.0, 0.0)
    above = lax.broadcasted_iota(jnp.int32, (rows, rows), 0) > lax.broadcasted_iota(
        jnp.int32, (rows, rows), 1
    )
    rank = jnp.dot(
        jnp.where(above, 1.0, 0.0).astype(BF16), member.astype(BF16), preferred_element_type=F32
    )
    rank = jnp.where(member > 0.5, rank, -1.0).astype(BF16)
    weight = jnp.zeros(member.shape, F32)
    for k in range(TOP):
        weight = weight + jnp.where(found[k], routing_ref[:, TOP + k : TOP + k + 1], 0.0)
    high = weight.astype(BF16)
    low = (weight - high.astype(F32)).astype(BF16)
    at = 0
    for first, count in parts:
        slots = experts * count

        def layout(dims, dim):
            slot = lax.broadcasted_iota(jnp.int32, dims, dim).astype(F32)
            expert = jnp.floor((slot + 0.5) * (1.0 / count))
            return expert, slot - expert * count + first

        expert, place = layout((slots, rows), 0)
        expert_column = layout((slots, experts), 0)[0]
        columns = lax.broadcasted_iota(jnp.int32, (slots, experts), 1).astype(F32)
        select = jnp.where(expert_column == columns, 1.0, 0.0).astype(BF16)
        wanted = lax.dot_general(select, rank, NT, preferred_element_type=F32)
        pick_ref[at : at + slots, :] = jnp.where(wanted == place, 1.0, 0.0).astype(BF16)
        expert_row = layout((experts, slots), 1)[0]
        lines = lax.broadcasted_iota(jnp.int32, (experts, slots), 0).astype(F32)
        select = jnp.where(expert_row == lines, 1.0, 0.0).astype(BF16)
        mine = jnp.dot(rank, select, preferred_element_type=F32) == layout((rows, slots), 1)[1]
        for part, target in ((high, high_ref), (low, low_ref)):
            spread = jnp.dot(part, select, preferred_element_type=F32)
            target[:, at : at + slots] = jnp.where(mine, spread, 0.0).astype(BF16)
        at += slots


def project_kernel(count, attn_ref, residual_ref, gain_ref, router_ref, pick_ref, *refs):
    pieces, refs = refs[:count], refs[count:]
    normed_out, state_out, slots_out, normed_rows, state, picked, sems = refs
    step = 512
    square = jnp.zeros((attn_ref.shape[0], 1), F32)
    moves = []

    def move(source, target, kind, at, size=step):
        window = (slice(None), pl.ds(at, size))
        moves.append(pltpu.make_async_copy(source.at[window], target.at[window], sems.at[kind, at // step]))
        moves[-1].start()

    for at in range(0, D, step):
        cols = slice(at, at + step)
        part = residual_ref[:, cols].astype(F32)
        row = 0
        for piece in pieces:
            deep = piece.shape[0]
            part = part + jnp.dot(
                attn_ref[:, row : row + deep], piece[:, cols], preferred_element_type=F32
            )
            row += deep
        state[:, cols] = part
        move(state, state_out, 0, at)
        square = square + jnp.sum(part * part, axis=1, keepdims=True)
    factor = lax.rsqrt(square * (1.0 / D) + EPSILON)
    logit = jnp.zeros_like(square)
    for at in range(0, D, step):
        cols = slice(at, at + step)
        normed = (state[:, cols] * factor * gain_ref[:, cols]).astype(BF16)
        normed_rows[:, cols] = normed
        move(normed_rows, normed_out, 2, at)
        logit = logit + jnp.sum(
            normed.astype(F32) * router_ref[:, cols].astype(F32), axis=1, keepdims=True
        )
        picked[:, cols] = jnp.dot(pick_ref[...], normed, preferred_element_type=F32).astype(BF16)
        move(picked, slots_out, 1, at)
    state[:, D:] = jnp.broadcast_to(jax.nn.sigmoid(logit), (state.shape[0], HD))
    move(state, state_out, 0, D, HD)
    for copy in moves:
        copy.wait()


def ffn_kernel(xs, shards, outs, *refs):
    x_refs, refs = refs[:xs], refs[xs:]
    sources, refs = [refs[kind * shards : (kind + 1) * shards] for kind in range(3)], refs[3 * shards :]
    out_refs, refs = refs[:outs], refs[outs:]
    x, *weights, hidden, result, sems = refs
    gate, up, down = weights
    chunk = 256
    hid = gate.shape[0]
    steps = [(at, min(chunk, hid - at)) for at in range(0, hid, chunk)]
    x_copies = []
    at = 0
    for number, ref in enumerate(x_refs):
        x_copies.append(pltpu.make_async_copy(ref, x.at[pl.ds(at, ref.shape[0])], sems.at[4, number]))
        at += ref.shape[0]
    size = hid // shards
    loads = [(shard, first) for shard in range(shards) for first in range(0, size, size if shards > 1 else chunk)]
    copies = [[], [], []]
    ends = []
    for number, (shard, first) in enumerate(loads):
        count = size if shards > 1 else min(chunk, size - first)
        ends.append(shard * size + first + count)
        for kind in range(3):
            copies[kind].append(
                pltpu.make_async_copy(
                    sources[kind][shard].at[pl.ds(first, count)],
                    weights[kind].at[pl.ds(shard * size + first, count)],
                    sems.at[kind, number],
                )
            )
    for copy in x_copies:
        copy.start()
    for pair in zip(copies[0], copies[1]):
        for copy in pair:
            copy.start()
    for copy in copies[2]:
        copy.start()
    for copy in x_copies:
        copy.wait()
    ready = 0
    for first, count in steps:
        while ready < len(ends) and (ready == 0 or ends[ready - 1] < first + count):
            copies[0][ready].wait()
            copies[1][ready].wait()
            ready += 1
        rows = slice(first, first + count)
        g = lax.dot_general(x[...], gate[rows, :], NT, preferred_element_type=F32)
        u = lax.dot_general(x[...], up[rows, :], NT, preferred_element_type=F32)
        hidden[:, rows] = (g / (1.0 + jnp.exp(-g)) * u).astype(BF16)
    for copy in copies[2]:
        copy.wait()
    moves = []
    for number, at in enumerate(range(0, D, chunk)):
        cols = slice(at, at + chunk)
        result[:, cols] = jnp.dot(hidden[...], down[:, cols], preferred_element_type=F32).astype(BF16)
        row = 0
        for ref in out_refs:
            moves.append(
                pltpu.make_async_copy(
                    result.at[pl.ds(row, ref.shape[0]), pl.ds(at, chunk)],
                    ref.at[:, pl.ds(at, chunk)],
                    sems.at[3 if row == 0 else 5, number],
                )
            )
            moves[-1].start()
            row += ref.shape[0]
    for move in moves:
        move.wait()


def ffn(x_list, weights, out_rows):
    rows = sum(x.shape[0] for x in x_list)
    hid = sum(w.shape[0] for w in weights[0])
    spec = ANY if len(weights[0]) > 1 else HBM
    return pl.pallas_call(
        functools.partial(ffn_kernel, len(x_list), len(weights[0]), len(out_rows)),
        out_shape=[jax.ShapeDtypeStruct((n, D), BF16) for n in out_rows],
        in_specs=[ANY] * len(x_list) + [spec] * (3 * len(weights[0])),
        out_specs=[HBM] * len(out_rows),
        scratch_shapes=[
            pltpu.VMEM((rows, D), BF16),
            pltpu.VMEM((hid, D), BF16),
            pltpu.VMEM((hid, D), BF16),
            pltpu.VMEM((hid, D), BF16),
            pltpu.VMEM((rows, hid), BF16),
            pltpu.VMEM((rows, D), BF16),
            pltpu.SemaphoreType.DMA((6, 8)),
        ],
        compiler_params=pltpu.CompilerParams(vmem_limit_bytes=56 << 20),
        cost_estimate=pl.CostEstimate(
            flops=6 * rows * hid * D, bytes_accessed=6 * hid * D + 4 * rows * D, transcendentals=rows * hid
        ),
    )(*x_list, *weights[0], *weights[1], *weights[2])


def combine_kernel(count, high_ref, low_ref, *refs):
    sources, out_ref, refs = refs[:count], refs[count], refs[count + 1 :]
    held, result, sems = refs[:count], refs[count], refs[count + 1]
    rows = result.shape[0]
    loads = []
    for number, (source, target) in enumerate(zip(sources, held)):
        loads.append(pltpu.make_async_copy(source.at[pl.ds(0, target.shape[0])], target, sems.at[0, number]))
        loads[-1].start()
    for load in loads:
        load.wait()
    state, keep, sib, far, back, *relayed = held
    scale = state[:, D : D + 1]
    step = 512
    moves = []
    for at in range(0, D, step):
        cols = slice(at, at + step)
        routed = jnp.dot(high_ref[...], back[:, cols], preferred_element_type=F32) + jnp.dot(
            low_ref[...], back[:, cols], preferred_element_type=F32
        )
        for ref in relayed:
            routed = routed + ref[:, cols].astype(F32)
        shared = keep[:, cols].astype(F32) + sib[:, cols].astype(F32) + far[:, cols].astype(F32)
        result[:, cols] = (state[:, cols] + scale * shared + routed).astype(BF16)
        window = (pl.ds(0, rows), pl.ds(at, step))
        moves.append(pltpu.make_async_copy(result.at[window], out_ref.at[window], sems.at[1, at // step]))
        moves[-1].start()
    for move in moves:
        move.wait()


def pick_kernel(pick_ref, rows_ref, out_ref, picked, sems):
    step = 512
    moves = []
    for at in range(0, D, step):
        cols = slice(at, at + step)
        picked[:, cols] = jnp.dot(pick_ref[...], rows_ref[:, cols], preferred_element_type=F32).astype(BF16)
        window = (slice(None), pl.ds(at, step))
        moves.append(pltpu.make_async_copy(picked.at[window], out_ref.at[window], sems.at[at // step]))
        moves[-1].start()
    for move in moves:
        move.wait()


def relay_kernel(high_ref, low_ref, back_ref, out_ref):
    step = 512
    for at in range(0, D, step):
        cols = slice(at, at + step)
        back = back_ref[:, cols]
        routed = jnp.dot(high_ref[...], back, preferred_element_type=F32) + jnp.dot(
            low_ref[...], back, preferred_element_type=F32
        )
        out_ref[:, cols] = routed.astype(BF16)


def vmem_call(kernel, out_shape, specs, limit=8, scratch=(), flops=0):
    return pl.pallas_call(
        kernel,
        out_shape=out_shape,
        in_specs=specs,
        out_specs=jax.tree.map(lambda _: VMEM, out_shape),
        scratch_shapes=scratch,
        compiler_params=pltpu.CompilerParams(vmem_limit_bytes=limit << 20),
        cost_estimate=pl.CostEstimate(flops=flops, bytes_accessed=4 << 20, transcendentals=0),
    )


def shape(*dims, dtype=BF16):
    return jax.ShapeDtypeStruct(dims, dtype)


def grp_move(array, flip):
    return lax.ppermute(array, "grp", [(i, i ^ flip) for i in range(lax.axis_size("grp"))])


def req_shift(array, distance):
    devices = range(lax.axis_size("req"))
    return lax.ppermute(array, "req", [(i - distance, i) for i in devices if i - distance in devices])


def pack_kernel(ring_0, ring_1, ring_2, ring_3, first_ref, second_ref):
    half = ring_0.shape[0] // 2
    for number, ref in enumerate((ring_0, ring_1, ring_2, ring_3)):
        first_ref[number * half : (number + 1) * half, :] = ref[:half, :]
        second_ref[number * half : (number + 1) * half, :] = ref[half:, :]


def join_kernel(first_ref, first_far, second_ref, second_far, first_out, second_out):
    rows = second_ref.shape[0]
    first_out[:rows, :] = first_ref[...]
    first_out[rows:, :] = first_far[...]
    second_out[:rows, :] = second_ref[...]
    second_out[rows:, :] = second_far[...]


def over_y(array):
    return lax.ppermute(array, "req", [(i, i ^ 1) for i in range(8)])


def order_kernel(place_ref, out_ref):
    total = out_ref.shape[0]
    part = total // 32
    half = part // 2
    req, grp = place_ref[0], place_ref[1]
    step = 128
    for piece in range(8):
        index = lax.broadcasted_iota(jnp.int32, (1, step), 1)
        flip = lax.shift_right_logical(index, int(math.log2(4 * half))) & 1
        turn = lax.shift_right_logical(index, int(math.log2(half))) & 3
        far, swapped = piece // 2 % 2, piece % 2
        y_flip, x_flip = (far, flip) if swapped else (flip, far)
        row = ((req + 8 - 2 * turn) & 7) ^ y_flip
        column = grp ^ (2 * x_flip + piece // 4)
        target = (row * 4 + column) * part + swapped * half + (index & (half - 1))
        lines = lax.broadcasted_iota(jnp.int32, (total, step), 0)
        out_ref[:, piece * step : (piece + 1) * step] = jnp.where(lines == target, 1.0, 0.0).astype(BF16)


def gather_ring(array):
    return [array] + [
        lax.ppermute(array, "req", [(i, (i + 2 * d) % 8) for i in range(8)]) for d in range(1, 4)
    ]


def local(
    suffix_queries,
    suffix_keys,
    suffix_values,
    prefix_cache,
    residual,
    out_weight,
    norm_gain,
    routes,
    route_weights,
    lengths,
    migrate,
    expert_gate,
    expert_up,
    expert_down,
    shared_gate,
    shared_up,
    shared_down,
    shared_router,
):
    rows = suffix_queries.shape[1]
    requests = lax.axis_size("req")
    req = lax.axis_index("req")
    grp = lax.axis_index("grp")
    depth = min(8, requests // 4)
    prefix_len = prefix_cache.shape[1] * requests
    capacity = rows * TOP * 5 // (4 * requests)
    place = jnp.stack([req, grp]).astype(jnp.int32)

    inverse = ROPE_BASE ** (-2.0 * np.arange(HD // 2) / HD)
    inverse = jnp.asarray(np.concatenate([inverse, inverse])[None].astype(np.float32))
    query_turned, own_cache = vmem_call(
        functools.partial(rope_kernel, prefix_len),
        [shape(rows, WIDTH), shape(rows, 2 * WIDTH)],
        [SMEM, SMEM] + [VMEM] * 4,
    )(lengths, place, inverse, suffix_queries[0], suffix_keys[0], suffix_values[0])

    routing = jnp.concatenate([routes[0].astype(F32), route_weights[0]], axis=1)
    halves = requests == 8
    experts = requests // 2 if halves else requests
    base = (req // experts * experts).astype(jnp.int32)[None]
    slots = experts * capacity

    def route(table):
        return vmem_call(
            functools.partial(route_kernel, experts, [(0, capacity)]),
            [shape(slots, rows), shape(rows, slots), shape(rows, slots)],
            [SMEM, VMEM],
        )(base, table)

    def across(array):
        return lax.ppermute(array, "req", [(i, i ^ requests // 2) for i in range(requests)])

    pick, high, low = route(routing)

    def attend(prefix_rows, history, order):
        return vmem_call(
            functools.partial(attend_kernel, depth),
            shape(rows, WIDTH),
            [SMEM, SMEM] + [VMEM] * (3 + depth + len(order)),
            flops=ATTEND_COST,
        )(lengths, place, query_turned, prefix_rows, own_cache, *history, *order)

    mine = [jnp.swapaxes(expert_gate[0], 0, 1), jnp.swapaxes(expert_up[0], 0, 1), expert_down[0]]
    part = prefix_cache[0].reshape(-1, HD)
    prefix_rows = lax.all_to_all(
        jnp.broadcast_to(part[None], (requests, *part.shape)), "req", split_axis=0, concat_axis=0, tiled=True
    ).reshape(prefix_len, 2 * WIDTH)
    if halves:
        far_routing = across(routing)
        half = out_weight.shape[0] // 2
        ring = gather_ring(out_weight)
        far_gate = grp_move(mine[0], 2)
        *ring, late_cache, late_up, far_gate, far_routing, prefix_rows = lax.optimization_barrier(
            (*ring, own_cache, mine[1], far_gate, far_routing, prefix_rows)
        )
        first, second = vmem_call(pack_kernel, [shape(4 * half, D), shape(4 * half, D)], [VMEM] * 4)(*ring)
        first, second, late_cache = lax.optimization_barrier((first, second, late_cache))
        first_far, second_far = over_y(first), grp_move(second, 2)
        history = [req_shift(late_cache, distance) for distance in range(1, depth + 1)]
        far_pick, far_high, far_low = route(far_routing)
        order = vmem_call(order_kernel, shape(WIDTH, WIDTH), [SMEM])(place)
        far_up = grp_move(late_up, 2)
        first_far, second_far, order, pick, far_pick, far_up = lax.optimization_barrier(
            (first_far, second_far, order, pick, far_pick, far_up)
        )
        first, second = vmem_call(
            join_kernel, [shape(8 * half, D), shape(8 * half, D)], [VMEM] * 4
        )(first, first_far, second, second_far)
        attention = attend(prefix_rows, history, [order])
        near = [first, second, grp_move(first, 1), grp_move(second, 1)]
        far = [grp_move(first, 2), over_y(second)]
        *far, attention, late_down = lax.optimization_barrier((*far, attention, mine[2]))
        pieces = near[:2] + far + near[2:] + [grp_move(array, 1) for array in far]
        far_down = grp_move(late_down, 2)
    else:
        pieces = [lax.all_gather(out_weight, ("req", "grp"), axis=0, tiled=True)]
        history = [req_shift(own_cache, distance) for distance in range(1, depth + 1)]
        attention = attend(prefix_rows, history, [])
        far_gate, far_up, far_down = [grp_move(w, 2) for w in mine]

    normed, state, outgoing = pl.pallas_call(
        functools.partial(project_kernel, len(pieces)),
        out_shape=[shape(rows, D), shape(rows, D + HD, dtype=F32), shape(slots, D)],
        in_specs=[VMEM] * (5 + len(pieces)),
        out_specs=[HBM] * 3,
        scratch_shapes=[
            pltpu.VMEM((rows, D), BF16),
            pltpu.VMEM((rows, D + HD), F32),
            pltpu.VMEM((slots, D), BF16),
            pltpu.SemaphoreType.DMA((3, 5)),
        ],
        compiler_params=pltpu.CompilerParams(vmem_limit_bytes=16 << 20),
        cost_estimate=pl.CostEstimate(flops=2 * rows * WIDTH * D, bytes_accessed=8 << 20, transcendentals=0),
    )(attention, residual[0], norm_gain[None], shared_router[None], pick, *pieces)

    groups = [list(range(at, at + experts)) for at in range(0, requests, experts)] if halves else None

    def exchange(array):
        split = array.reshape(experts, capacity, D)
        return lax.all_to_all(
            split, "req", split_axis=0, concat_axis=0, axis_index_groups=groups, tiled=True
        ).reshape(slots, D)

    def both(own, other):
        return [own, grp_move(own, 1), other, grp_move(other, 1)]

    gates, ups = both(mine[0], far_gate), both(mine[1], far_up)
    arrived = exchange(outgoing)
    late_normed, late_cache, far_rows = normed, own_cache, None
    if halves:
        relay_rows = across(normed)
        relay_rows, arrived, late_normed, far_down, gates, ups = lax.optimization_barrier(
            (relay_rows, arrived, normed, far_down, gates, ups)
        )
        relay_out = pl.pallas_call(
            pick_kernel,
            out_shape=shape(slots, D),
            in_specs=[VMEM] * 2,
            out_specs=HBM,
            scratch_shapes=[pltpu.VMEM((slots, D), BF16), pltpu.SemaphoreType.DMA((4,))],
        )(far_pick, relay_rows)
        relay_arrived = exchange(relay_out)
    weights = [gates, ups, both(mine[2], far_down)]
    far_rows = grp_move(late_normed, 2)
    (finished,) = ffn([arrived], weights, [slots])
    if halves:
        relay_arrived, finished, late_cache, far_rows = lax.optimization_barrier(
            (relay_arrived, finished, own_cache, far_rows)
        )
        (relay_finished,) = ffn([relay_arrived], weights, [slots])
        relay_back = exchange(relay_finished)
        relay_finished, normed, far_rows = lax.optimization_barrier((relay_finished, normed, far_rows))
    keep, send = ffn(
        [normed, far_rows, grp_move(normed, 1), grp_move(far_rows, 1)],
        [[jnp.swapaxes(shared_gate, 0, 1)], [jnp.swapaxes(shared_up, 0, 1)], [shared_down]],
        [2 * rows, 2 * rows],
    )
    partner = grp_move(late_cache, 2)
    if halves:
        relay_back, partner, finished, keep, send = lax.optimization_barrier(
            (relay_back, partner, finished, keep, send)
        )
    from_sib = grp_move(send, 1)
    pair_sum = (keep[rows:].astype(F32) + from_sib[rows:].astype(F32)).astype(BF16)
    from_far = grp_move(pair_sum, 2)
    relayed = []
    if halves:
        relay_sum = vmem_call(relay_kernel, shape(rows, D), [VMEM] * 3)(far_high, far_low, relay_back)
        relayed = [across(relay_sum)]
    back = exchange(finished)

    sources = [state, keep, from_sib, from_far, back, *relayed]
    kept = [(rows, D + HD)] + [(rows, D)] * 3 + [(slots, D)] + [(rows, D)] * len(relayed)
    final = pl.pallas_call(
        functools.partial(combine_kernel, len(sources)),
        out_shape=shape(rows, D),
        in_specs=[VMEM] * 2 + [ANY] * len(sources),
        out_specs=HBM,
        scratch_shapes=[pltpu.VMEM(dims, source.dtype) for dims, source in zip(kept, sources)]
        + [pltpu.VMEM((rows, D), BF16), pltpu.SemaphoreType.DMA((2, 8))],
        compiler_params=pltpu.CompilerParams(vmem_limit_bytes=32 << 20),
        cost_estimate=pl.CostEstimate(flops=4 * slots * rows * D, bytes_accessed=8 << 20, transcendentals=0),
    )(high, low, *sources)

    pair_row = grp // 4 * 2 + grp % 2
    flags = jnp.sum(
        jnp.where((jnp.arange(migrate.shape[0], dtype=jnp.int32) == pair_row)[:, None], migrate, 0), axis=0
    )
    page_moved = jnp.repeat(flags, PG) == 1
    suffix_cache = jnp.where(page_moved[:, None], partner, own_cache)
    return (final[None], suffix_cache[None])


def solution(mesh):
    placed = (
        P("grp", "req", None),
        P("grp", "req", None),
        P("grp", "req", None),
        P("grp", "req", None),
        P("grp", "req", None),
        P(("req", "grp"), None),
        P(),
        P("grp", "req", None),
        P("grp", "req", None),
        P("grp", None),
        P(None, "req"),
        P("req", None, "grp"),
        P("req", None, "grp"),
        P("req", "grp", None),
        P(None, "grp"),
        P(None, "grp"),
        P("grp", None),
        P(),
    )
    return jax.shard_map(
        local,
        mesh=mesh,
        in_specs=placed,
        out_specs=(P("grp", "req", None), P("grp", "req", None)),
        check_vma=False,
    )
```

```python
import functools
import math

import jax
import jax.numpy as jnp
import numpy as np
from jax import lax
from jax.experimental import pallas as pl
from jax.experimental.pallas import tpu as pltpu
from jax.sharding import PartitionSpec as P

D = 2048
HD = 128
HEADS = 8
WIDTH = HEADS * HD
TOP = 4
PG = 16
ROPE_BASE = 1000000.0
EPSILON = 1e-06
ATTEND_COST = 20_000_000_000
F32 = jnp.float32
BF16 = jnp.bfloat16
VMEM = pl.BlockSpec(memory_space=pltpu.VMEM)
SMEM = pl.BlockSpec(memory_space=pltpu.SMEM)
HBM = pl.BlockSpec(memory_space=pltpu.HBM)
ANY = pl.BlockSpec(memory_space=pl.ANY)
NT = (((1,), (1,)), ((), ()))


def request_starts(lengths_ref, token_ids):
    start = jnp.zeros_like(token_ids)
    end = jnp.int32(0)
    for request in range(lengths_ref.shape[1]):
        end = end + lengths_ref[0, request]
        start = jnp.where(token_ids >= end, end, start)
    return start


def rope_kernel(prefix_len, lengths_ref, place_ref, inv_ref, q_ref, k_ref, v_ref, turned_ref, cache_ref):
    rows = q_ref.shape[0]
    shape = (rows, HD)
    token_ids = place_ref[0] * rows + lax.broadcasted_iota(jnp.int32, shape, 0)
    offset = token_ids - request_starts(lengths_ref, token_ids)
    angles = (prefix_len + offset).astype(F32) * inv_ref[...]
    cosine = jnp.cos(angles)
    sine = jnp.sin(angles)
    sine = jnp.where(lax.broadcasted_iota(jnp.int32, shape, 1) < HD // 2, -sine, sine)
    for head in range(HEADS):
        cols = slice(head * HD, (head + 1) * HD)
        for source, target in ((q_ref, turned_ref), (k_ref, cache_ref)):
            entries = source[:, cols].astype(F32)
            turned = entries * cosine + pltpu.roll(entries, HD // 2, 1) * sine
            target[:, cols] = turned.astype(BF16)
    cache_ref[:, WIDTH:] = v_ref[...]


def attend_kernel(depth, lengths_ref, place_ref, q_ref, prefix_ref, *refs):
    blocks, order, out_ref = refs[: depth + 1], refs[depth + 1 : -1], refs[-1]
    rows = q_ref.shape[0]
    prefix_len = prefix_ref.shape[0]
    first = place_ref[0] * rows
    ids = lax.broadcasted_iota(jnp.int32, (rows, rows), 0) + first
    start = request_starts(lengths_ref, ids)
    allowed = [jnp.ones((rows, prefix_len), jnp.bool_)]
    for distance in range(depth + 1):
        keys = lax.broadcasted_iota(jnp.int32, (rows, rows), 1) + (first - distance * rows)
        allowed.append((keys <= ids) & (keys >= start))
    bias = jnp.concatenate([jnp.where(a, 0.0, -1e30) for a in allowed], axis=1)
    keep = bias == 0.0
    sources = (prefix_ref,) + blocks
    for head in range(HEADS):
        cols = slice(head * HD, (head + 1) * HD)
        values_at = slice(WIDTH + head * HD, WIDTH + (head + 1) * HD)
        keys = jnp.concatenate([s[:, cols] for s in sources], axis=0)
        values = jnp.concatenate([s[:, values_at] for s in sources], axis=0)
        scores = lax.dot_general(q_ref[:, cols], keys, NT, preferred_element_type=F32)
        scores = jnp.where(keep, scores * HD ** (-0.5), -1e30)
        highest = jnp.max(scores, axis=1, keepdims=True)
        weights = jnp.where(keep, jnp.exp(scores - highest), 0.0)
        total = jnp.sum(weights, axis=1, keepdims=True)
        blended = jnp.dot(weights.astype(BF16), values, preferred_element_type=F32) / total
        out_ref[:, cols] = blended.astype(BF16)
    if order:
        out_ref[...] = jnp.dot(out_ref[...], order[0][...], preferred_element_type=F32).astype(BF16)


def fill_table(routes_ref, weights_ref):
    weights = weights_ref[...]
    high = weights.astype(BF16)
    low = (weights - high.astype(F32)).astype(BF16)
    parts = [routes_ref[...].astype(F32), high.astype(F32), low.astype(F32), jnp.zeros(weights.shape, F32)]
    return jnp.concatenate(parts, axis=0).astype(BF16)


def table_kernel(routes_ref, weights_ref, table_ref):
    table_ref[...] = fill_table(routes_ref, weights_ref)


def near_kernel(weight_ref, prefix_ref, routes_ref, weights_ref, near_ref, table_ref):
    table = fill_table(routes_ref, weights_ref)
    table_ref[...] = table
    rows = weight_ref.shape[0]
    near_ref[:, :D] = weight_ref[...]
    count = rows // prefix_ref.shape[0]
    narrow = D // count
    lines = lax.broadcasted_iota(jnp.int32, (rows, prefix_ref.shape[0]), 0)
    columns = lax.broadcasted_iota(jnp.int32, (rows, prefix_ref.shape[0]), 1) * count
    prefix = jnp.zeros((rows, narrow), F32)
    for number in range(count):
        spot = jnp.where(lines == columns + number, 1.0, 0.0).astype(BF16)
        prefix = prefix + jnp.dot(
            spot, prefix_ref[:, number * narrow : (number + 1) * narrow], preferred_element_type=F32
        )
    near_ref[:, D : D + narrow] = prefix.astype(BF16)
    near_ref[: 4 * TOP, D + narrow :] = table
    near_ref[4 * TOP :, D + narrow :] = jnp.zeros((rows - 4 * TOP, table.shape[1]), BF16)


def route_kernel(experts, parts, relative, halves, place_ref, table_ref, pick_ref, high_ref, low_ref):
    rows = table_ref.shape[1]
    unit = jnp.where(
        lax.broadcasted_iota(jnp.int32, (4 * TOP, 4 * TOP), 0) == lax.broadcasted_iota(jnp.int32, (4 * TOP, 4 * TOP), 1),
        1.0,
        0.0,
    ).astype(BF16)
    routing = lax.dot_general(table_ref[...], unit, (((0,), (0,)), ((), ())), preferred_element_type=F32)
    plain = lax.broadcasted_iota(jnp.int32, (rows, experts), 1)
    above = lax.broadcasted_iota(jnp.int32, (rows, rows), 0) > lax.broadcasted_iota(
        jnp.int32, (rows, rows), 1
    )
    above = jnp.where(above, 1.0, 0.0).astype(BF16)

    def places(turned):
        numbers = plain
        if halves:
            numbers = plain ^ place_ref[0] if turned else plain + (place_ref[0] & -experts)
        found = [routing[:, k : k + 1] == numbers.astype(F32) for k in range(TOP)]
        member = jnp.where(found[0] | found[1] | found[2] | found[3], 1.0, 0.0)
        rank = jnp.dot(above, member.astype(BF16), preferred_element_type=F32)
        return found, jnp.where(member > 0.5, rank, -1.0).astype(BF16)

    _, pick_rank = places(relative)
    found, rank = places(not relative)
    high, low = [
        sum(jnp.where(found[k], routing[:, at + k : at + k + 1], 0.0) for k in range(TOP)).astype(BF16)
        for at in (TOP, 2 * TOP)
    ]
    at = 0
    for first, count in parts:
        slots = experts * count

        def layout(dims, dim):
            slot = lax.broadcasted_iota(jnp.int32, dims, dim).astype(F32)
            expert = jnp.floor((slot + 0.5) * (1.0 / count))
            return expert, slot - expert * count + first

        expert, place = layout((slots, rows), 0)
        expert_column = layout((slots, experts), 0)[0]
        columns = lax.broadcasted_iota(jnp.int32, (slots, experts), 1).astype(F32)
        select = jnp.where(expert_column == columns, 1.0, 0.0).astype(BF16)
        wanted = lax.dot_general(select, pick_rank, NT, preferred_element_type=F32)
        pick_ref[at : at + slots, :] = jnp.where(wanted == place, 1.0, 0.0).astype(BF16)
        expert_row = layout((experts, slots), 1)[0]
        lines = lax.broadcasted_iota(jnp.int32, (experts, slots), 0).astype(F32)
        select = jnp.where(expert_row == lines, 1.0, 0.0).astype(BF16)
        mine = jnp.dot(rank, select, preferred_element_type=F32) == layout((rows, slots), 1)[1]
        for part, target in ((high, high_ref), (low, low_ref)):
            spread = jnp.dot(part, select, preferred_element_type=F32)
            target[:, at : at + slots] = jnp.where(mine, spread, 0.0).astype(BF16)
        at += slots


def project_kernel(count, attn_ref, residual_ref, gain_ref, router_ref, pick_ref, *refs):
    pieces, refs = refs[:count], refs[count:]
    normed_out, state_out, *slots_out, normed_rows, state, picked, sems = refs
    step = 512
    square = jnp.zeros((attn_ref.shape[0], 1), F32)
    moves = []

    def move(source, target, kind, at, size=step):
        window = (slice(None), pl.ds(at, size))
        moves.append(pltpu.make_async_copy(source.at[window], target.at[window], sems.at[kind, at // step]))
        moves[-1].start()

    for at in range(0, D, step):
        cols = slice(at, at + step)
        part = residual_ref[:, cols].astype(F32)
        row = 0
        for piece in pieces:
            deep = piece.shape[0]
            part = part + jnp.dot(
                attn_ref[:, row : row + deep], piece[:, cols], preferred_element_type=F32
            )
            row += deep
        state[:, cols] = part
        move(state, state_out, 0, at)
        square = square + jnp.sum(part * part, axis=1, keepdims=True)
    factor = lax.rsqrt(square * (1.0 / D) + EPSILON)
    logit = jnp.zeros_like(square)
    for at in range(0, D, step):
        cols = slice(at, at + step)
        normed = (state[:, cols] * factor * gain_ref[:, cols]).astype(BF16)
        normed_rows[:, cols] = normed
        move(normed_rows, normed_out, 2, at)
        logit = logit + jnp.sum(
            normed.astype(F32) * router_ref[:, cols].astype(F32), axis=1, keepdims=True
        )
        picked[:, cols] = jnp.dot(pick_ref[...], normed, preferred_element_type=F32).astype(BF16)
        row = 0
        for number, ref in enumerate(slots_out):
            move(picked.at[pl.ds(row, ref.shape[0])], ref, 3 + number, at)
            row += ref.shape[0]
    state[:, D:] = jnp.broadcast_to(jax.nn.sigmoid(logit), (state.shape[0], HD))
    move(state, state_out, 0, D, HD)
    for copy in moves:
        copy.wait()


def ffn_kernel(xs, shards, outs, turn, place_ref, *refs):
    x_refs, refs = refs[:xs], refs[xs:]
    sources, refs = [refs[kind * shards : (kind + 1) * shards] for kind in range(3)], refs[3 * shards :]
    out_refs, refs = refs[:outs], refs[outs:]
    x, *weights, hidden, result, sems, out_sems = refs
    gate, up, down = weights
    chunk = 256
    hid = gate.shape[0]
    steps = [(at, min(chunk, hid - at)) for at in range(0, hid, chunk)]
    x_copies = []
    at = 0
    for number, ref in enumerate(x_refs):
        x_copies.append(pltpu.make_async_copy(ref, x.at[pl.ds(at, ref.shape[0])], sems.at[4, number]))
        at += ref.shape[0]
    size = hid // shards
    loads = [(shard, first) for shard in range(shards) for first in range(0, size, size if shards > 1 else chunk)]
    copies = [[], [], []]
    ends = []
    for number, (shard, first) in enumerate(loads):
        count = size if shards > 1 else min(chunk, size - first)
        ends.append(shard * size + first + count)
        for kind in range(3):
            copies[kind].append(
                pltpu.make_async_copy(
                    sources[kind][shard].at[pl.ds(first, count)],
                    weights[kind].at[pl.ds(shard * size + first, count)],
                    sems.at[kind, number],
                )
            )
    for copy in x_copies:
        copy.start()
    for pair in zip(copies[0], copies[1]):
        for copy in pair:
            copy.start()
    for copy in copies[2]:
        copy.start()
    for copy in x_copies:
        copy.wait()
    ready = 0
    for first, count in steps:
        while ready < len(ends) and (ready == 0 or ends[ready - 1] < first + count):
            copies[0][ready].wait()
            copies[1][ready].wait()
            ready += 1
        rows = slice(first, first + count)
        g = lax.dot_general(x[...], gate[rows, :], NT, preferred_element_type=F32)
        u = lax.dot_general(x[...], up[rows, :], NT, preferred_element_type=F32)
        hidden[:, rows] = (g / (1.0 + jnp.exp(-g)) * u).astype(BF16)
    for copy in copies[2]:
        copy.wait()
    moves = []
    size_of = x.shape[0] // max(turn, 1)
    for number, at in enumerate(range(0, D, chunk)):
        cols = slice(at, at + chunk)
        result[:, cols] = jnp.dot(hidden[...], down[:, cols], preferred_element_type=F32).astype(BF16)
        row = 0
        for block in range(max(turn, outs)):
            if turn:
                other = pl.multiple_of(((place_ref[0] & (turn - 1)) ^ block) * size_of, size_of)
                if outs > 1:
                    source, first, target = other, 0, out_refs[block]
                else:
                    source, first, target = block * size_of, other, out_refs[0]
                count = size_of
            else:
                source, first, target = row, 0, out_refs[block]
                count = target.shape[0]
                row += count
            moves.append(
                pltpu.make_async_copy(
                    result.at[pl.ds(source, count), pl.ds(at, chunk)],
                    target.at[pl.ds(first, count), pl.ds(at, chunk)],
                    out_sems.at[block, number],
                )
            )
            moves[-1].start()
    for move in moves:
        move.wait()


def ffn(x_list, weights, out_rows, place, turn=0):
    rows = sum(x.shape[0] for x in x_list)
    hid = sum(w.shape[0] for w in weights[0])
    spec = ANY if len(weights[0]) > 1 else HBM
    return pl.pallas_call(
        functools.partial(ffn_kernel, len(x_list), len(weights[0]), len(out_rows), turn),
        out_shape=[jax.ShapeDtypeStruct((n, D), BF16) for n in out_rows],
        in_specs=[SMEM] + [ANY] * len(x_list) + [spec] * (3 * len(weights[0])),
        out_specs=[HBM] * len(out_rows),
        scratch_shapes=[
            pltpu.VMEM((rows, D), BF16),
            pltpu.VMEM((hid, D), BF16),
            pltpu.VMEM((hid, D), BF16),
            pltpu.VMEM((hid, D), BF16),
            pltpu.VMEM((rows, hid), BF16),
            pltpu.VMEM((rows, D), BF16),
            pltpu.SemaphoreType.DMA((5, 8)),
            pltpu.SemaphoreType.DMA((max(turn, len(out_rows)), 8)),
        ],
        compiler_params=pltpu.CompilerParams(vmem_limit_bytes=56 << 20),
        cost_estimate=pl.CostEstimate(
            flops=6 * rows * hid * D, bytes_accessed=6 * hid * D + 4 * rows * D, transcendentals=rows * hid
        ),
    )(place, *x_list, *weights[0], *weights[1], *weights[2])


def combine_kernel(count, backs, high_ref, low_ref, *refs):
    sources, out_ref, refs = refs[:count], refs[count], refs[count + 1 :]
    *held, back, result, sems = refs
    rows = result.shape[0]
    targets = list(held)
    row = 0
    for source in sources[count - backs :]:
        targets.append(back.at[pl.ds(row, source.shape[0])])
        row += source.shape[0]
    loads = []
    for number, (source, target) in enumerate(zip(sources, targets)):
        loads.append(pltpu.make_async_copy(source.at[pl.ds(0, target.shape[0])], target, sems.at[0, number]))
        loads[-1].start()
    for load in loads:
        load.wait()
    state, keep, sib, far, *relayed = held
    scale = state[:, D : D + 1]
    step = 512
    moves = []
    for at in range(0, D, step):
        cols = slice(at, at + step)
        routed = jnp.dot(high_ref[...], back[:, cols], preferred_element_type=F32) + jnp.dot(
            low_ref[...], back[:, cols], preferred_element_type=F32
        )
        for ref in relayed:
            routed = routed + ref[:, cols].astype(F32)
        shared = keep[:, cols].astype(F32) + sib[:, cols].astype(F32) + far[:, cols].astype(F32)
        result[:, cols] = (state[:, cols] + scale * shared + routed).astype(BF16)
        window = (pl.ds(0, rows), pl.ds(at, step))
        moves.append(pltpu.make_async_copy(result.at[window], out_ref.at[window], sems.at[1, at // step]))
        moves[-1].start()
    for move in moves:
        move.wait()


def pick_kernel(pick_ref, rows_ref, *refs):
    *out_refs, picked, sems = refs
    step = 512
    moves = []
    for at in range(0, D, step):
        cols = slice(at, at + step)
        picked[:, cols] = jnp.dot(pick_ref[...], rows_ref[:, cols], preferred_element_type=F32).astype(BF16)
        row = 0
        for number, ref in enumerate(out_refs):
            source = picked.at[pl.ds(row, ref.shape[0]), pl.ds(at, step)]
            moves.append(pltpu.make_async_copy(source, ref.at[:, pl.ds(at, step)], sems.at[number, at // step]))
            moves[-1].start()
            row += ref.shape[0]
    for move in moves:
        move.wait()


def relay_kernel(high_ref, low_ref, *refs):
    sources, (out_ref, back, sems) = refs[:-3], refs[-3:]
    loads = []
    row = 0
    for number, ref in enumerate(sources):
        loads.append(pltpu.make_async_copy(ref, back.at[pl.ds(row, ref.shape[0])], sems.at[number]))
        loads[-1].start()
        row += ref.shape[0]
    for load in loads:
        load.wait()
    step = 512
    for at in range(0, D, step):
        cols = slice(at, at + step)
        routed = jnp.dot(high_ref[...], back[:, cols], preferred_element_type=F32) + jnp.dot(
            low_ref[...], back[:, cols], preferred_element_type=F32
        )
        out_ref[:, cols] = routed.astype(BF16)


def vmem_call(kernel, out_shape, specs, limit=8, scratch=(), flops=0):
    return pl.pallas_call(
        kernel,
        out_shape=out_shape,
        in_specs=specs,
        out_specs=jax.tree.map(lambda _: VMEM, out_shape),
        scratch_shapes=scratch,
        compiler_params=pltpu.CompilerParams(vmem_limit_bytes=limit << 20),
        cost_estimate=pl.CostEstimate(flops=flops, bytes_accessed=4 << 20, transcendentals=0),
    )


def shape(*dims, dtype=BF16):
    return jax.ShapeDtypeStruct(dims, dtype)


def grp_move(array, flip):
    return lax.ppermute(array, "grp", [(i, i ^ flip) for i in range(lax.axis_size("grp"))])


def req_shift(array, distance):
    devices = range(lax.axis_size("req"))
    return lax.ppermute(array, "req", [(i - distance, i) for i in devices if i - distance in devices])


def pack_kernel(ring_0, ring_1, ring_2, ring_3, first_ref, second_ref, table_ref):
    half = second_ref.shape[0] // 4
    ring = (ring_0, ring_1, ring_2, ring_3)
    narrow = ring_0.shape[1] - D - table_ref.shape[1]
    count = D // narrow
    for number, ref in enumerate(ring):
        first_ref[number * half : (number + 1) * half, :] = ref[:half, :D]
        second_ref[number * half : (number + 1) * half, :] = ref[half:, :D]
    table_ref[...] = ring_2[: 4 * TOP, D + narrow :]
    prefix = jnp.concatenate([ref[:, D : D + narrow] for ref in ring], axis=0)
    lines = lax.broadcasted_iota(jnp.int32, (half, prefix.shape[0]), 0) * count
    columns = lax.broadcasted_iota(jnp.int32, (half, prefix.shape[0]), 1)
    for number in range(count):
        spot = jnp.where(lines + number == columns, 1.0, 0.0).astype(BF16)
        first_ref[4 * half :, number * narrow : (number + 1) * narrow] = jnp.dot(
            spot, prefix, preferred_element_type=F32
        ).astype(BF16)


def join_kernel(first_ref, first_far, second_ref, second_far, first_out, second_out, prefix_out):
    rows = second_ref.shape[0]
    first_out[:rows, :] = first_ref[:rows, :]
    first_out[rows:, :] = first_far[:rows, :]
    second_out[:rows, :] = second_ref[...]
    second_out[rows:, :] = second_far[...]
    half = prefix_out.shape[0] // 2
    prefix_out[:half, :] = first_ref[rows:, :]
    prefix_out[half:, :] = first_far[rows:, :]


def over_y(array):
    return lax.ppermute(array, "req", [(i, i ^ 1) for i in range(8)])


def order_kernel(place_ref, out_ref):
    total = out_ref.shape[0]
    part = total // 32
    half = part // 2
    req, grp = place_ref[0], place_ref[1]
    step = 128
    for piece in range(8):
        index = lax.broadcasted_iota(jnp.int32, (1, step), 1)
        flip = lax.shift_right_logical(index, int(math.log2(4 * half))) & 1
        turn = lax.shift_right_logical(index, int(math.log2(half))) & 3
        far, swapped = piece // 2 % 2, piece % 2
        y_flip, x_flip = (far, flip) if swapped else (flip, far)
        row = ((req + 8 - 2 * turn) & 7) ^ y_flip
        column = grp ^ (2 * x_flip + piece // 4)
        target = (row * 4 + column) * part + swapped * half + (index & (half - 1))
        lines = lax.broadcasted_iota(jnp.int32, (total, step), 0)
        out_ref[:, piece * step : (piece + 1) * step] = jnp.where(lines == target, 1.0, 0.0).astype(BF16)


def gather_ring(array):
    return [array] + [
        lax.ppermute(array, "req", [(i, (i + 2 * d) % 8) for i in range(8)]) for d in range(1, 4)
    ]


def local(
    suffix_queries,
    suffix_keys,
    suffix_values,
    prefix_cache,
    residual,
    out_weight,
    norm_gain,
    routes,
    route_weights,
    lengths,
    migrate,
    expert_gate,
    expert_up,
    expert_down,
    shared_gate,
    shared_up,
    shared_down,
    shared_router,
):
    rows = suffix_queries.shape[1]
    requests = lax.axis_size("req")
    req = lax.axis_index("req")
    grp = lax.axis_index("grp")
    depth = min(8, requests // 4)
    prefix_len = prefix_cache.shape[1] * requests
    capacity = rows * TOP * 5 // (4 * requests)
    place = jnp.stack([req, grp]).astype(jnp.int32)

    inverse = ROPE_BASE ** (-2.0 * np.arange(HD // 2) / HD)
    inverse = jnp.asarray(np.concatenate([inverse, inverse])[None].astype(np.float32))
    query_turned, own_cache = vmem_call(
        functools.partial(rope_kernel, prefix_len),
        [shape(rows, WIDTH), shape(rows, 2 * WIDTH)],
        [SMEM, SMEM] + [VMEM] * 4,
    )(lengths, place, inverse, suffix_queries[0], suffix_keys[0], suffix_values[0])

    halves = requests == 8
    experts = requests // 2 if halves else requests
    slots = experts * capacity

    def route(table, relative):
        return vmem_call(
            functools.partial(route_kernel, experts, [(0, capacity)], relative, halves),
            [shape(slots, rows), shape(rows, slots), shape(rows, slots)],
            [SMEM, VMEM],
        )(place, table)

    def across(array):
        return lax.ppermute(array, "req", [(i, i ^ requests // 2) for i in range(requests)])

    def attend(prefix_rows, history, order):
        return vmem_call(
            functools.partial(attend_kernel, depth),
            shape(rows, WIDTH),
            [SMEM, SMEM] + [VMEM] * (3 + depth + len(order)),
            flops=ATTEND_COST,
        )(lengths, place, query_turned, prefix_rows, own_cache, *history, *order)

    mine = [jnp.swapaxes(expert_gate[0], 0, 1), jnp.swapaxes(expert_up[0], 0, 1), expert_down[0]]
    tables = [jnp.swapaxes(routes[0], 0, 1), jnp.swapaxes(route_weights[0], 0, 1)]
    if halves:
        half = out_weight.shape[0] // 2
        extra = prefix_cache.shape[1] * D // out_weight.shape[0] + rows
        near, table = vmem_call(
            near_kernel, [shape(2 * half, D + extra), shape(4 * TOP, rows)], [VMEM] * 4
        )(out_weight, prefix_cache[0], *tables)
        ring = gather_ring(near)
        far_gate = grp_move(mine[0], 2)
        history = [req_shift(own_cache, 1)]
        *ring, late_cache, far_gate = lax.optimization_barrier((*ring, own_cache, far_gate))
        first, second, far_table = vmem_call(
            pack_kernel, [shape(5 * half, D), shape(4 * half, D), shape(4 * TOP, rows)], [VMEM] * 4
        )(*ring)
        first, second, late_cache = lax.optimization_barrier((first, second, late_cache))
        first_far, second_far = over_y(first), grp_move(second, 2)
        history += [req_shift(late_cache, distance) for distance in range(2, depth + 1)]
        pick, high, low = route(table, True)
        far_pick, far_high, far_low = route(far_table, False)
        order = vmem_call(order_kernel, shape(WIDTH, WIDTH), [SMEM])(place)
        first_far, second_far, order, pick, far_pick = lax.optimization_barrier(
            (first_far, second_far, order, pick, far_pick)
        )
        first, second, prefix_rows = vmem_call(
            join_kernel, [shape(8 * half, D), shape(8 * half, D), shape(2 * half, D)], [VMEM] * 4
        )(first, first_far, second, second_far)
        attention = attend(prefix_rows, history, [order])
        near = [first, second, grp_move(first, 1), grp_move(second, 1)]
        far = [grp_move(first, 2), over_y(second)]
        far, attention, late_up, late_down = lax.optimization_barrier((far, attention, mine[1], mine[2]))
        pieces = near[:2] + far + near[2:] + [grp_move(array, 1) for array in far]
        far_up, far_down = grp_move(late_up, 2), grp_move(late_down, 2)
    else:
        (table,) = vmem_call(table_kernel, [shape(4 * TOP, rows)], [VMEM] * 2)(*tables)
        pick, high, low = route(table, False)
        pieces = [lax.all_gather(out_weight, ("req", "grp"), axis=0, tiled=True)]
        prefix_rows = lax.all_gather(prefix_cache[0], "req", axis=0, tiled=True)
        history = [req_shift(own_cache, distance) for distance in range(1, depth + 1)]
        attention = attend(prefix_rows, history, [])
        far_gate, far_up, far_down = [grp_move(w, 2) for w in mine]

    shares = [capacity] * experts if halves else [slots]
    normed, state, *outgoing = pl.pallas_call(
        functools.partial(project_kernel, len(pieces)),
        out_shape=[shape(rows, D), shape(rows, D + HD, dtype=F32)] + [shape(n, D) for n in shares],
        in_specs=[VMEM] * (5 + len(pieces)),
        out_specs=[HBM] * (2 + len(shares)),
        scratch_shapes=[
            pltpu.VMEM((rows, D), BF16),
            pltpu.VMEM((rows, D + HD), F32),
            pltpu.VMEM((slots, D), BF16),
            pltpu.SemaphoreType.DMA((3 + len(shares), 5)),
        ],
        compiler_params=pltpu.CompilerParams(vmem_limit_bytes=16 << 20),
        cost_estimate=pl.CostEstimate(flops=2 * rows * WIDTH * D, bytes_accessed=8 << 20, transcendentals=0),
    )(attention, residual[0], norm_gain[None], shared_router[None], pick, *pieces)

    groups = [list(range(at, at + experts)) for at in range(0, requests, experts)] if halves else None

    def exchange(array):
        split = array.reshape(experts, capacity, D)
        return lax.all_to_all(
            split, "req", split_axis=0, concat_axis=0, axis_index_groups=groups, tiled=True
        ).reshape(slots, D)

    def trade(arrays):
        if not halves:
            return [exchange(arrays[0])]
        return [arrays[0]] + [
            lax.ppermute(array, "req", [(i, i ^ flip) for i in range(requests)])
            for flip, array in enumerate(arrays)
            if flip
        ]

    def both(own, other):
        return [own, grp_move(own, 1), other, grp_move(other, 1)]

    def shared(normed, far_rows):
        return ffn(
            [normed, far_rows, grp_move(normed, 1), grp_move(far_rows, 1)],
            [[jnp.swapaxes(shared_gate, 0, 1)], [jnp.swapaxes(shared_up, 0, 1)], [shared_down]],
            [2 * rows, 2 * rows],
            place,
        )

    def spread(send, keep):
        from_sib = grp_move(send, 1)
        pair_sum = (keep[rows:].astype(F32) + from_sib[rows:].astype(F32)).astype(BF16)
        return from_sib, grp_move(pair_sum, 2)

    def all_weights(*others):
        return [both(own, other) for own, other in zip(mine, others)]

    arrived = trade(outgoing)
    relayed = []
    if halves:
        relay_rows = across(normed)
        relay_rows, arrived, late_normed, far_gate, far_up, far_down, late_cache = lax.optimization_barrier(
            (relay_rows, arrived, normed, far_gate, far_up, far_down, own_cache)
        )
        (relay_out,) = pl.pallas_call(
            pick_kernel,
            out_shape=[shape(slots, D)],
            in_specs=[VMEM] * 2,
            out_specs=[HBM],
            scratch_shapes=[pltpu.VMEM((slots, D), BF16), pltpu.SemaphoreType.DMA((1, 4))],
        )(far_pick, relay_rows)
        relay_arrived = exchange(relay_out)
        far_rows = grp_move(late_normed, 2)
        weights = all_weights(far_gate, far_up, far_down)
        finished = ffn(arrived, weights, [slots], place, experts)
        relay_arrived, finished, far_rows, weights, late_cache = lax.optimization_barrier(
            (relay_arrived, finished, far_rows, weights, late_cache)
        )
        relay_finished = ffn([relay_arrived], weights, shares, place, experts)
        relay_back = trade(relay_finished)
        partner = grp_move(late_cache, 2)
        relay_finished, normed, far_rows = lax.optimization_barrier((relay_finished, normed, far_rows))
        keep, send = shared(normed, far_rows)
        relay_back, finished, keep, send, partner = lax.optimization_barrier(
            (relay_back, finished, keep, send, partner)
        )
        relay_sum = pl.pallas_call(
            relay_kernel,
            out_shape=shape(rows, D),
            in_specs=[VMEM] * 2 + [ANY] * experts,
            out_specs=VMEM,
            scratch_shapes=[pltpu.VMEM((slots, D), BF16), pltpu.SemaphoreType.DMA((experts,))],
            compiler_params=pltpu.CompilerParams(vmem_limit_bytes=32 << 20),
        )(far_high, far_low, *relay_back)
        relayed = [across(relay_sum)]
        from_sib, from_far = spread(send, keep)
    else:
        finished = ffn(arrived, all_weights(far_gate, far_up, far_down), shares, place)
        keep, send = shared(normed, grp_move(normed, 2))
        from_sib, from_far = spread(send, keep)
        partner = grp_move(own_cache, 2)
    back = [exchange(finished[0])]

    sources = [state, keep, from_sib, from_far, *relayed, *back]
    kept = [(rows, D + HD)] + [(rows, D)] * (3 + len(relayed)) + [(slots, D)]
    final = pl.pallas_call(
        functools.partial(combine_kernel, len(sources), len(back)),
        out_shape=shape(rows, D),
        in_specs=[VMEM] * 2 + [ANY] * len(sources),
        out_specs=HBM,
        scratch_shapes=[pltpu.VMEM(dims, source.dtype) for dims, source in zip(kept, sources)]
        + [pltpu.VMEM((rows, D), BF16), pltpu.SemaphoreType.DMA((2, 16))],
        compiler_params=pltpu.CompilerParams(vmem_limit_bytes=56 << 20),
        cost_estimate=pl.CostEstimate(flops=4 * slots * rows * D, bytes_accessed=8 << 20, transcendentals=0),
    )(high, low, *sources)

    pair_row = grp // 4 * 2 + grp % 2
    flags = jnp.sum(
        jnp.where((jnp.arange(migrate.shape[0], dtype=jnp.int32) == pair_row)[:, None], migrate, 0), axis=0
    )
    page_moved = jnp.repeat(flags, PG) == 1
    suffix_cache = jnp.where(page_moved[:, None], partner, own_cache)
    return (final[None], suffix_cache[None])


def solution(mesh):
    placed = (
        P("grp", "req", None),
        P("grp", "req", None),
        P("grp", "req", None),
        P("grp", "req", None),
        P("grp", "req", None),
        P(("req", "grp"), None),
        P(),
        P("grp", "req", None),
        P("grp", "req", None),
        P("grp", None),
        P(None, "req"),
        P("req", None, "grp"),
        P("req", None, "grp"),
        P("req", "grp", None),
        P(None, "grp"),
        P(None, "grp"),
        P("grp", None),
        P(),
    )
    return jax.shard_map(
        local,
        mesh=mesh,
        in_specs=placed,
        out_specs=(P("grp", "req", None), P("grp", "req", None)),
        check_vma=False,
    )
```

```python
import functools
import math

import jax
import jax.numpy as jnp
import numpy as np
from jax import lax
from jax.experimental import pallas as pl
from jax.experimental.pallas import tpu as pltpu
from jax.sharding import PartitionSpec as P

D = 2048
HD = 128
HEADS = 8
WIDTH = HEADS * HD
TOP = 4
PG = 16
ROPE_BASE = 1000000.0
EPSILON = 1e-06
ATTEND_COST = 20_000_000_000
F32 = jnp.float32
BF16 = jnp.bfloat16
VMEM = pl.BlockSpec(memory_space=pltpu.VMEM)
SMEM = pl.BlockSpec(memory_space=pltpu.SMEM)
HBM = pl.BlockSpec(memory_space=pltpu.HBM)
ANY = pl.BlockSpec(memory_space=pl.ANY)
NT = (((1,), (1,)), ((), ()))


def request_starts(lengths_ref, token_ids):
    start = jnp.zeros_like(token_ids)
    end = jnp.int32(0)
    for request in range(lengths_ref.shape[1]):
        end = end + lengths_ref[0, request]
        start = jnp.where(token_ids >= end, end, start)
    return start


def rope_kernel(prefix_len, lengths_ref, place_ref, inv_ref, q_ref, k_ref, v_ref, turned_ref, cache_ref):
    rows = q_ref.shape[0]
    shape = (rows, HD)
    token_ids = place_ref[0] * rows + lax.broadcasted_iota(jnp.int32, shape, 0)
    offset = token_ids - request_starts(lengths_ref, token_ids)
    angles = (prefix_len + offset).astype(F32) * inv_ref[...]
    cosine = jnp.cos(angles)
    sine = jnp.sin(angles)
    sine = jnp.where(lax.broadcasted_iota(jnp.int32, shape, 1) < HD // 2, -sine, sine)
    for head in range(HEADS):
        cols = slice(head * HD, (head + 1) * HD)
        for source, target in ((q_ref, turned_ref), (k_ref, cache_ref)):
            entries = source[:, cols].astype(F32)
            turned = entries * cosine + pltpu.roll(entries, HD // 2, 1) * sine
            target[:, cols] = turned.astype(BF16)
    cache_ref[:, WIDTH:] = v_ref[...]


def attend_kernel(depth, lengths_ref, place_ref, q_ref, prefix_ref, *refs):
    blocks, order, out_ref = refs[: depth + 1], refs[depth + 1 : -1], refs[-1]
    rows = q_ref.shape[0]
    prefix_len = prefix_ref.shape[0]
    first = place_ref[0] * rows
    ids = lax.broadcasted_iota(jnp.int32, (rows, rows), 0) + first
    start = request_starts(lengths_ref, ids)
    allowed = [jnp.ones((rows, prefix_len), jnp.bool_)]
    for distance in range(depth + 1):
        keys = lax.broadcasted_iota(jnp.int32, (rows, rows), 1) + (first - distance * rows)
        allowed.append((keys <= ids) & (keys >= start))
    bias = jnp.concatenate([jnp.where(a, 0.0, -1e30) for a in allowed], axis=1)
    keep = bias == 0.0
    sources = (prefix_ref,) + blocks
    for head in range(HEADS):
        cols = slice(head * HD, (head + 1) * HD)
        values_at = slice(WIDTH + head * HD, WIDTH + (head + 1) * HD)
        keys = jnp.concatenate([s[:, cols] for s in sources], axis=0)
        values = jnp.concatenate([s[:, values_at] for s in sources], axis=0)
        scores = lax.dot_general(q_ref[:, cols], keys, NT, preferred_element_type=F32)
        scores = jnp.where(keep, scores * HD ** (-0.5), -1e30)
        highest = jnp.max(scores, axis=1, keepdims=True)
        weights = jnp.where(keep, jnp.exp(scores - highest), 0.0)
        total = jnp.sum(weights, axis=1, keepdims=True)
        blended = jnp.dot(weights.astype(BF16), values, preferred_element_type=F32) / total
        out_ref[:, cols] = blended.astype(BF16)
    if order:
        out_ref[...] = jnp.dot(out_ref[...], order[0][...], preferred_element_type=F32).astype(BF16)


def fill_table(routes_ref, weights_ref):
    weights = weights_ref[...]
    high = weights.astype(BF16)
    low = (weights - high.astype(F32)).astype(BF16)
    parts = [routes_ref[...].astype(F32), high.astype(F32), low.astype(F32), jnp.zeros(weights.shape, F32)]
    return jnp.concatenate(parts, axis=0).astype(BF16)


def table_kernel(routes_ref, weights_ref, table_ref):
    table_ref[...] = fill_table(routes_ref, weights_ref)


def near_kernel(weight_ref, prefix_ref, routes_ref, weights_ref, near_ref, table_ref):
    table = fill_table(routes_ref, weights_ref)
    table_ref[...] = table
    rows = weight_ref.shape[0]
    near_ref[:, :D] = weight_ref[...]
    count = rows // prefix_ref.shape[0]
    narrow = D // count
    lines = lax.broadcasted_iota(jnp.int32, (rows, prefix_ref.shape[0]), 0)
    columns = lax.broadcasted_iota(jnp.int32, (rows, prefix_ref.shape[0]), 1) * count
    prefix = jnp.zeros((rows, narrow), F32)
    for number in range(count):
        spot = jnp.where(lines == columns + number, 1.0, 0.0).astype(BF16)
        prefix = prefix + jnp.dot(
            spot, prefix_ref[:, number * narrow : (number + 1) * narrow], preferred_element_type=F32
        )
    near_ref[:, D : D + narrow] = prefix.astype(BF16)
    near_ref[: 4 * TOP, D + narrow :] = table
    near_ref[4 * TOP :, D + narrow :] = jnp.zeros((rows - 4 * TOP, table.shape[1]), BF16)


def route_kernel(experts, parts, relative, halves, place_ref, table_ref, pick_ref, high_ref, low_ref):
    rows = table_ref.shape[1]
    unit = jnp.where(
        lax.broadcasted_iota(jnp.int32, (4 * TOP, 4 * TOP), 0) == lax.broadcasted_iota(jnp.int32, (4 * TOP, 4 * TOP), 1),
        1.0,
        0.0,
    ).astype(BF16)
    routing = lax.dot_general(table_ref[...], unit, (((0,), (0,)), ((), ())), preferred_element_type=F32)
    plain = lax.broadcasted_iota(jnp.int32, (rows, experts), 1)
    above = lax.broadcasted_iota(jnp.int32, (rows, rows), 0) > lax.broadcasted_iota(
        jnp.int32, (rows, rows), 1
    )
    above = jnp.where(above, 1.0, 0.0).astype(BF16)

    def places(turned):
        numbers = plain
        if halves:
            numbers = plain ^ place_ref[0] if turned else plain + (place_ref[0] & -experts)
        found = [routing[:, k : k + 1] == numbers.astype(F32) for k in range(TOP)]
        member = jnp.where(found[0] | found[1] | found[2] | found[3], 1.0, 0.0)
        rank = jnp.dot(above, member.astype(BF16), preferred_element_type=F32)
        return found, jnp.where(member > 0.5, rank, -1.0).astype(BF16)

    _, pick_rank = places(relative)
    found, rank = places(not relative)
    high, low = [
        sum(jnp.where(found[k], routing[:, at + k : at + k + 1], 0.0) for k in range(TOP)).astype(BF16)
        for at in (TOP, 2 * TOP)
    ]
    at = 0
    for first, count in parts:
        slots = experts * count

        def layout(dims, dim):
            slot = lax.broadcasted_iota(jnp.int32, dims, dim).astype(F32)
            expert = jnp.floor((slot + 0.5) * (1.0 / count))
            return expert, slot - expert * count + first

        expert, place = layout((slots, rows), 0)
        expert_column = layout((slots, experts), 0)[0]
        columns = lax.broadcasted_iota(jnp.int32, (slots, experts), 1).astype(F32)
        select = jnp.where(expert_column == columns, 1.0, 0.0).astype(BF16)
        wanted = lax.dot_general(select, pick_rank, NT, preferred_element_type=F32)
        pick_ref[at : at + slots, :] = jnp.where(wanted == place, 1.0, 0.0).astype(BF16)
        expert_row = layout((experts, slots), 1)[0]
        lines = lax.broadcasted_iota(jnp.int32, (experts, slots), 0).astype(F32)
        select = jnp.where(expert_row == lines, 1.0, 0.0).astype(BF16)
        mine = jnp.dot(rank, select, preferred_element_type=F32) == layout((rows, slots), 1)[1]
        for part, target in ((high, high_ref), (low, low_ref)):
            spread = jnp.dot(part, select, preferred_element_type=F32)
            target[:, at : at + slots] = jnp.where(mine, spread, 0.0).astype(BF16)
        at += slots


def project_kernel(count, attn_ref, residual_ref, gain_ref, router_ref, pick_ref, *refs):
    pieces, refs = refs[:count], refs[count:]
    normed_out, state_out, *slots_out, normed_rows, state, picked, sems = refs
    step = 512
    square = jnp.zeros((attn_ref.shape[0], 1), F32)
    moves = []

    def move(source, target, kind, at, size=step):
        window = (slice(None), pl.ds(at, size))
        moves.append(pltpu.make_async_copy(source.at[window], target.at[window], sems.at[kind, at // step]))
        moves[-1].start()

    for at in range(0, D, step):
        cols = slice(at, at + step)
        part = residual_ref[:, cols].astype(F32)
        row = 0
        for piece in pieces:
            deep = piece.shape[0]
            part = part + jnp.dot(
                attn_ref[:, row : row + deep], piece[:, cols], preferred_element_type=F32
            )
            row += deep
        state[:, cols] = part
        move(state, state_out, 0, at)
        square = square + jnp.sum(part * part, axis=1, keepdims=True)
    factor = lax.rsqrt(square * (1.0 / D) + EPSILON)
    logit = jnp.zeros_like(square)
    for at in range(0, D, step):
        cols = slice(at, at + step)
        normed = (state[:, cols] * factor * gain_ref[:, cols]).astype(BF16)
        normed_rows[:, cols] = normed
        move(normed_rows, normed_out, 2, at)
        logit = logit + jnp.sum(
            normed.astype(F32) * router_ref[:, cols].astype(F32), axis=1, keepdims=True
        )
        picked[:, cols] = jnp.dot(pick_ref[...], normed, preferred_element_type=F32).astype(BF16)
        row = 0
        for number, ref in enumerate(slots_out):
            move(picked.at[pl.ds(row, ref.shape[0])], ref, 3 + number, at)
            row += ref.shape[0]
    state[:, D:] = jnp.broadcast_to(jax.nn.sigmoid(logit), (state.shape[0], HD))
    move(state, state_out, 0, D, HD)
    for copy in moves:
        copy.wait()


def ffn_kernel(xs, shards, outs, turn, place_ref, *refs):
    x_refs, refs = refs[:xs], refs[xs:]
    sources, refs = [refs[kind * shards : (kind + 1) * shards] for kind in range(3)], refs[3 * shards :]
    out_refs, refs = refs[:outs], refs[outs:]
    x, *weights, hidden, result, sems, out_sems = refs
    gate, up, down = weights
    chunk = 256
    hid = gate.shape[0]
    steps = [(at, min(chunk, hid - at)) for at in range(0, hid, chunk)]
    x_copies = []
    at = 0
    for number, ref in enumerate(x_refs):
        x_copies.append(pltpu.make_async_copy(ref, x.at[pl.ds(at, ref.shape[0])], sems.at[4, number]))
        at += ref.shape[0]
    size = hid // shards
    loads = [(shard, first) for shard in range(shards) for first in range(0, size, size if shards > 1 else chunk)]
    copies = [[], [], []]
    ends = []
    for number, (shard, first) in enumerate(loads):
        count = size if shards > 1 else min(chunk, size - first)
        ends.append(shard * size + first + count)
        for kind in range(3):
            copies[kind].append(
                pltpu.make_async_copy(
                    sources[kind][shard].at[pl.ds(first, count)],
                    weights[kind].at[pl.ds(shard * size + first, count)],
                    sems.at[kind, number],
                )
            )
    for copy in x_copies:
        copy.start()
    for pair in zip(copies[0], copies[1]):
        for copy in pair:
            copy.start()
    for copy in copies[2]:
        copy.start()
    for copy in x_copies:
        copy.wait()
    ready = 0
    for first, count in steps:
        while ready < len(ends) and (ready == 0 or ends[ready - 1] < first + count):
            copies[0][ready].wait()
            copies[1][ready].wait()
            ready += 1
        rows = slice(first, first + count)
        g = lax.dot_general(x[...], gate[rows, :], NT, preferred_element_type=F32)
        u = lax.dot_general(x[...], up[rows, :], NT, preferred_element_type=F32)
        hidden[:, rows] = (g / (1.0 + jnp.exp(-g)) * u).astype(BF16)
    for copy in copies[2]:
        copy.wait()
    moves = []
    size_of = x.shape[0] // max(turn, 1)
    for number, at in enumerate(range(0, D, chunk)):
        cols = slice(at, at + chunk)
        result[:, cols] = jnp.dot(hidden[...], down[:, cols], preferred_element_type=F32).astype(BF16)
        row = 0
        for block in range(max(turn, outs)):
            if turn:
                other = pl.multiple_of(((place_ref[0] & (turn - 1)) ^ block) * size_of, size_of)
                if outs > 1:
                    source, first, target = other, 0, out_refs[block]
                else:
                    source, first, target = block * size_of, other, out_refs[0]
                count = size_of
            else:
                source, first, target = row, 0, out_refs[block]
                count = target.shape[0]
                row += count
            moves.append(
                pltpu.make_async_copy(
                    result.at[pl.ds(source, count), pl.ds(at, chunk)],
                    target.at[pl.ds(first, count), pl.ds(at, chunk)],
                    out_sems.at[block, number],
                )
            )
            moves[-1].start()
    for move in moves:
        move.wait()


def ffn(x_list, weights, out_rows, place, turn=0):
    rows = sum(x.shape[0] for x in x_list)
    hid = sum(w.shape[0] for w in weights[0])
    spec = ANY if len(weights[0]) > 1 else HBM
    return pl.pallas_call(
        functools.partial(ffn_kernel, len(x_list), len(weights[0]), len(out_rows), turn),
        out_shape=[jax.ShapeDtypeStruct((n, D), BF16) for n in out_rows],
        in_specs=[SMEM] + [ANY] * len(x_list) + [spec] * (3 * len(weights[0])),
        out_specs=[HBM] * len(out_rows),
        scratch_shapes=[
            pltpu.VMEM((rows, D), BF16),
            pltpu.VMEM((hid, D), BF16),
            pltpu.VMEM((hid, D), BF16),
            pltpu.VMEM((hid, D), BF16),
            pltpu.VMEM((rows, hid), BF16),
            pltpu.VMEM((rows, D), BF16),
            pltpu.SemaphoreType.DMA((5, 8)),
            pltpu.SemaphoreType.DMA((max(turn, len(out_rows)), 8)),
        ],
        compiler_params=pltpu.CompilerParams(vmem_limit_bytes=56 << 20),
        cost_estimate=pl.CostEstimate(
            flops=6 * rows * hid * D, bytes_accessed=6 * hid * D + 4 * rows * D, transcendentals=rows * hid
        ),
    )(place, *x_list, *weights[0], *weights[1], *weights[2])


def blend_kernel(state_hbm, keep_hbm, sib_hbm, far_hbm, out_ref, state, keep, sib, far, sems):
    loads = []
    for number, (source, target) in enumerate(((state_hbm, state), (keep_hbm, keep), (sib_hbm, sib), (far_hbm, far))):
        loads.append(pltpu.make_async_copy(source.at[pl.ds(0, target.shape[0])], target, sems.at[number]))
        loads[-1].start()
    for load in loads:
        load.wait()
    step = 512
    for at in range(0, D, step):
        cols = slice(at, at + step)
        shared = keep[:, cols].astype(F32) + sib[:, cols].astype(F32) + far[:, cols].astype(F32)
        out_ref[:, cols] = state[:, cols] + state[:, D : D + 1] * shared


def combine_kernel(count, backs, high_ref, low_ref, blend_ref, *refs):
    sources, out_ref, refs = refs[:count], refs[count], refs[count + 1 :]
    *relayed, back, result, sems = refs
    rows = result.shape[0]
    targets = list(relayed)
    row = 0
    for source in sources[count - backs :]:
        targets.append(back.at[pl.ds(row, source.shape[0])])
        row += source.shape[0]
    loads = []
    for number, (source, target) in enumerate(zip(sources, targets)):
        loads.append(pltpu.make_async_copy(source, target, sems.at[0, number]))
        loads[-1].start()
    for load in loads:
        load.wait()
    step = 512
    moves = []
    for at in range(0, D, step):
        cols = slice(at, at + step)
        routed = jnp.dot(high_ref[...], back[:, cols], preferred_element_type=F32) + jnp.dot(
            low_ref[...], back[:, cols], preferred_element_type=F32
        )
        for ref in relayed:
            routed = routed + ref[:, cols].astype(F32)
        result[:, cols] = (blend_ref[:, cols] + routed).astype(BF16)
        window = (pl.ds(0, rows), pl.ds(at, step))
        moves.append(pltpu.make_async_copy(result.at[window], out_ref.at[window], sems.at[1, at // step]))
        moves[-1].start()
    for move in moves:
        move.wait()


def pick_kernel(pick_ref, rows_ref, *refs):
    *out_refs, picked, sems = refs
    step = 512
    moves = []
    for at in range(0, D, step):
        cols = slice(at, at + step)
        picked[:, cols] = jnp.dot(pick_ref[...], rows_ref[:, cols], preferred_element_type=F32).astype(BF16)
        row = 0
        for number, ref in enumerate(out_refs):
            source = picked.at[pl.ds(row, ref.shape[0]), pl.ds(at, step)]
            moves.append(pltpu.make_async_copy(source, ref.at[:, pl.ds(at, step)], sems.at[number, at // step]))
            moves[-1].start()
            row += ref.shape[0]
    for move in moves:
        move.wait()


def relay_kernel(high_ref, low_ref, *refs):
    sources, (out_ref, back, sems) = refs[:-3], refs[-3:]
    loads = []
    row = 0
    for number, ref in enumerate(sources):
        loads.append(pltpu.make_async_copy(ref, back.at[pl.ds(row, ref.shape[0])], sems.at[number]))
        loads[-1].start()
        row += ref.shape[0]
    for load in loads:
        load.wait()
    step = 512
    for at in range(0, D, step):
        cols = slice(at, at + step)
        routed = jnp.dot(high_ref[...], back[:, cols], preferred_element_type=F32) + jnp.dot(
            low_ref[...], back[:, cols], preferred_element_type=F32
        )
        out_ref[:, cols] = routed.astype(BF16)


def vmem_call(kernel, out_shape, specs, limit=8, scratch=(), flops=0):
    return pl.pallas_call(
        kernel,
        out_shape=out_shape,
        in_specs=specs,
        out_specs=jax.tree.map(lambda _: VMEM, out_shape),
        scratch_shapes=scratch,
        compiler_params=pltpu.CompilerParams(vmem_limit_bytes=limit << 20),
        cost_estimate=pl.CostEstimate(flops=flops, bytes_accessed=4 << 20, transcendentals=0),
    )


def shape(*dims, dtype=BF16):
    return jax.ShapeDtypeStruct(dims, dtype)


def grp_move(array, flip):
    return lax.ppermute(array, "grp", [(i, i ^ flip) for i in range(lax.axis_size("grp"))])


def req_shift(array, distance):
    devices = range(lax.axis_size("req"))
    return lax.ppermute(array, "req", [(i - distance, i) for i in devices if i - distance in devices])


def pack_kernel(ring_0, ring_1, ring_2, ring_3, first_ref, second_ref, table_ref):
    half = second_ref.shape[0] // 4
    ring = (ring_0, ring_1, ring_2, ring_3)
    narrow = ring_0.shape[1] - D - table_ref.shape[1]
    count = D // narrow
    for number, ref in enumerate(ring):
        first_ref[number * half : (number + 1) * half, :] = ref[:half, :D]
        second_ref[number * half : (number + 1) * half, :] = ref[half:, :D]
    table_ref[...] = ring_2[: 4 * TOP, D + narrow :]
    prefix = jnp.concatenate([ref[:, D : D + narrow] for ref in ring], axis=0)
    lines = lax.broadcasted_iota(jnp.int32, (half, prefix.shape[0]), 0) * count
    columns = lax.broadcasted_iota(jnp.int32, (half, prefix.shape[0]), 1)
    for number in range(count):
        spot = jnp.where(lines + number == columns, 1.0, 0.0).astype(BF16)
        first_ref[4 * half :, number * narrow : (number + 1) * narrow] = jnp.dot(
            spot, prefix, preferred_element_type=F32
        ).astype(BF16)


def join_kernel(first_ref, first_far, second_ref, second_far, first_out, second_out, prefix_out):
    rows = second_ref.shape[0]
    first_out[:rows, :] = first_ref[:rows, :]
    first_out[rows:, :] = first_far[:rows, :]
    second_out[:rows, :] = second_ref[...]
    second_out[rows:, :] = second_far[...]
    half = prefix_out.shape[0] // 2
    prefix_out[:half, :] = first_ref[rows:, :]
    prefix_out[half:, :] = first_far[rows:, :]


def over_y(array):
    return lax.ppermute(array, "req", [(i, i ^ 1) for i in range(8)])


def order_kernel(place_ref, out_ref):
    total = out_ref.shape[0]
    part = total // 32
    half = part // 2
    req, grp = place_ref[0], place_ref[1]
    step = 128
    for piece in range(8):
        index = lax.broadcasted_iota(jnp.int32, (1, step), 1)
        flip = lax.shift_right_logical(index, int(math.log2(4 * half))) & 1
        turn = lax.shift_right_logical(index, int(math.log2(half))) & 3
        far, swapped = piece // 2 % 2, piece % 2
        y_flip, x_flip = (far, flip) if swapped else (flip, far)
        row = ((req + 8 - 2 * turn) & 7) ^ y_flip
        column = grp ^ (2 * x_flip + piece // 4)
        target = (row * 4 + column) * part + swapped * half + (index & (half - 1))
        lines = lax.broadcasted_iota(jnp.int32, (total, step), 0)
        out_ref[:, piece * step : (piece + 1) * step] = jnp.where(lines == target, 1.0, 0.0).astype(BF16)


def gather_ring(array):
    return [array] + [
        lax.ppermute(array, "req", [(i, (i + 2 * d) % 8) for i in range(8)]) for d in range(1, 4)
    ]


def local(
    suffix_queries,
    suffix_keys,
    suffix_values,
    prefix_cache,
    residual,
    out_weight,
    norm_gain,
    routes,
    route_weights,
    lengths,
    migrate,
    expert_gate,
    expert_up,
    expert_down,
    shared_gate,
    shared_up,
    shared_down,
    shared_router,
):
    rows = suffix_queries.shape[1]
    requests = lax.axis_size("req")
    req = lax.axis_index("req")
    grp = lax.axis_index("grp")
    depth = min(8, requests // 4)
    prefix_len = prefix_cache.shape[1] * requests
    capacity = rows * TOP * 5 // (4 * requests)
    place = jnp.stack([req, grp]).astype(jnp.int32)

    inverse = ROPE_BASE ** (-2.0 * np.arange(HD // 2) / HD)
    inverse = jnp.asarray(np.concatenate([inverse, inverse])[None].astype(np.float32))
    query_turned, own_cache = vmem_call(
        functools.partial(rope_kernel, prefix_len),
        [shape(rows, WIDTH), shape(rows, 2 * WIDTH)],
        [SMEM, SMEM] + [VMEM] * 4,
    )(lengths, place, inverse, suffix_queries[0], suffix_keys[0], suffix_values[0])

    halves = requests == 8
    experts = requests // 2 if halves else requests
    slots = experts * capacity

    def route(table, relative):
        return vmem_call(
            functools.partial(route_kernel, experts, [(0, capacity)], relative, halves),
            [shape(slots, rows), shape(rows, slots), shape(rows, slots)],
            [SMEM, VMEM],
        )(place, table)

    def across(array):
        return lax.ppermute(array, "req", [(i, i ^ requests // 2) for i in range(requests)])

    def attend(prefix_rows, history, order):
        return vmem_call(
            functools.partial(attend_kernel, depth),
            shape(rows, WIDTH),
            [SMEM, SMEM] + [VMEM] * (3 + depth + len(order)),
            flops=ATTEND_COST,
        )(lengths, place, query_turned, prefix_rows, own_cache, *history, *order)

    mine = [jnp.swapaxes(expert_gate[0], 0, 1), jnp.swapaxes(expert_up[0], 0, 1), expert_down[0]]
    tables = [jnp.swapaxes(routes[0], 0, 1), jnp.swapaxes(route_weights[0], 0, 1)]
    if halves:
        half = out_weight.shape[0] // 2
        extra = prefix_cache.shape[1] * D // out_weight.shape[0] + rows
        near, table = vmem_call(
            near_kernel, [shape(2 * half, D + extra), shape(4 * TOP, rows)], [VMEM] * 4
        )(out_weight, prefix_cache[0], *tables)
        ring = gather_ring(near)
        far_gate = grp_move(mine[0], 2)
        history = [req_shift(own_cache, 1)]
        *ring, late_cache, far_gate = lax.optimization_barrier((*ring, own_cache, far_gate))
        first, second, far_table = vmem_call(
            pack_kernel, [shape(5 * half, D), shape(4 * half, D), shape(4 * TOP, rows)], [VMEM] * 4
        )(*ring)
        first, second, late_cache = lax.optimization_barrier((first, second, late_cache))
        first_far, second_far = over_y(first), grp_move(second, 2)
        history += [req_shift(late_cache, distance) for distance in range(2, depth + 1)]
        pick, high, low = route(table, True)
        far_pick, far_high, far_low = route(far_table, False)
        order = vmem_call(order_kernel, shape(WIDTH, WIDTH), [SMEM])(place)
        first_far, second_far, order, pick, far_pick = lax.optimization_barrier(
            (first_far, second_far, order, pick, far_pick)
        )
        first, second, prefix_rows = vmem_call(
            join_kernel, [shape(8 * half, D), shape(8 * half, D), shape(2 * half, D)], [VMEM] * 4
        )(first, first_far, second, second_far)
        attention = attend(prefix_rows, history, [order])
        near = [first, second, grp_move(first, 1), grp_move(second, 1)]
        far = [grp_move(first, 2), over_y(second)]
        far, attention, late_up, late_down = lax.optimization_barrier((far, attention, mine[1], mine[2]))
        pieces = near[:2] + far + near[2:] + [grp_move(array, 1) for array in far]
        far_up, far_down = grp_move(late_up, 2), grp_move(late_down, 2)
    else:
        (table,) = vmem_call(table_kernel, [shape(4 * TOP, rows)], [VMEM] * 2)(*tables)
        pick, high, low = route(table, False)
        pieces = [lax.all_gather(out_weight, ("req", "grp"), axis=0, tiled=True)]
        prefix_rows = lax.all_gather(prefix_cache[0], "req", axis=0, tiled=True)
        history = [req_shift(own_cache, distance) for distance in range(1, depth + 1)]
        attention = attend(prefix_rows, history, [])
        far_gate, far_up, far_down = [grp_move(w, 2) for w in mine]

    shares = [capacity] * experts if halves else [slots]
    normed, state, *outgoing = pl.pallas_call(
        functools.partial(project_kernel, len(pieces)),
        out_shape=[shape(rows, D), shape(rows, D + HD, dtype=F32)] + [shape(n, D) for n in shares],
        in_specs=[VMEM] * (5 + len(pieces)),
        out_specs=[HBM] * (2 + len(shares)),
        scratch_shapes=[
            pltpu.VMEM((rows, D), BF16),
            pltpu.VMEM((rows, D + HD), F32),
            pltpu.VMEM((slots, D), BF16),
            pltpu.SemaphoreType.DMA((3 + len(shares), 5)),
        ],
        compiler_params=pltpu.CompilerParams(vmem_limit_bytes=16 << 20),
        cost_estimate=pl.CostEstimate(flops=2 * rows * WIDTH * D, bytes_accessed=8 << 20, transcendentals=0),
    )(attention, residual[0], norm_gain[None], shared_router[None], pick, *pieces)

    groups = [list(range(at, at + experts)) for at in range(0, requests, experts)] if halves else None

    def exchange(array):
        split = array.reshape(experts, capacity, D)
        return lax.all_to_all(
            split, "req", split_axis=0, concat_axis=0, axis_index_groups=groups, tiled=True
        ).reshape(slots, D)

    def trade(arrays):
        if not halves:
            return [exchange(arrays[0])]
        return [arrays[0]] + [
            lax.ppermute(array, "req", [(i, i ^ flip) for i in range(requests)])
            for flip, array in enumerate(arrays)
            if flip
        ]

    def both(own, other):
        return [own, grp_move(own, 1), other, grp_move(other, 1)]

    def shared(normed, far_rows):
        return ffn(
            [normed, far_rows, grp_move(normed, 1), grp_move(far_rows, 1)],
            [[jnp.swapaxes(shared_gate, 0, 1)], [jnp.swapaxes(shared_up, 0, 1)], [shared_down]],
            [2 * rows, 2 * rows],
            place,
        )

    def spread(send, keep):
        from_sib = grp_move(send, 1)
        pair_sum = (keep[rows:].astype(F32) + from_sib[rows:].astype(F32)).astype(BF16)
        return from_sib, grp_move(pair_sum, 2)

    def all_weights(*others):
        return [both(own, other) for own, other in zip(mine, others)]

    arrived = trade(outgoing)
    relayed = []
    if halves:
        relay_rows = across(normed)
        relay_rows, arrived, late_normed, far_gate, far_up, far_down, late_cache = lax.optimization_barrier(
            (relay_rows, arrived, normed, far_gate, far_up, far_down, own_cache)
        )
        (relay_out,) = pl.pallas_call(
            pick_kernel,
            out_shape=[shape(slots, D)],
            in_specs=[VMEM] * 2,
            out_specs=[HBM],
            scratch_shapes=[pltpu.VMEM((slots, D), BF16), pltpu.SemaphoreType.DMA((1, 4))],
            compiler_params=pltpu.CompilerParams(vmem_limit_bytes=8 << 20),
        )(far_pick, relay_rows)
        relay_arrived = exchange(relay_out)
        far_rows = grp_move(late_normed, 2)
        weights = all_weights(far_gate, far_up, far_down)
        finished = ffn(arrived, weights, [slots], place, experts)
        relay_arrived, finished, far_rows, weights, late_cache = lax.optimization_barrier(
            (relay_arrived, finished, far_rows, weights, late_cache)
        )
        relay_finished = ffn([relay_arrived], weights, shares, place, experts)
        relay_back = trade(relay_finished)
        partner = grp_move(late_cache, 2)
        relay_finished, normed, far_rows = lax.optimization_barrier((relay_finished, normed, far_rows))
        keep, send = shared(normed, far_rows)
        relay_back, keep, send, partner = lax.optimization_barrier((relay_back, keep, send, partner))
        relay_sum = pl.pallas_call(
            relay_kernel,
            out_shape=shape(rows, D),
            in_specs=[VMEM] * 2 + [ANY] * experts,
            out_specs=VMEM,
            scratch_shapes=[pltpu.VMEM((slots, D), BF16), pltpu.SemaphoreType.DMA((experts,))],
            compiler_params=pltpu.CompilerParams(vmem_limit_bytes=32 << 20),
        )(far_high, far_low, *relay_back)
        relayed = [across(relay_sum)]
        from_sib, from_far = spread(send, keep)
    else:
        finished = ffn(arrived, all_weights(far_gate, far_up, far_down), shares, place)
        keep, send = shared(normed, grp_move(normed, 2))
        from_sib, from_far = spread(send, keep)
        partner = grp_move(own_cache, 2)
    back = [exchange(finished[0])]

    blend = pl.pallas_call(
        blend_kernel,
        out_shape=shape(rows, D, dtype=F32),
        in_specs=[ANY] * 4,
        out_specs=VMEM,
        scratch_shapes=[pltpu.VMEM((rows, D + HD), F32)]
        + [pltpu.VMEM((rows, D), BF16)] * 3
        + [pltpu.SemaphoreType.DMA((4,))],
        compiler_params=pltpu.CompilerParams(vmem_limit_bytes=56 << 20),
        cost_estimate=pl.CostEstimate(flops=4 * rows * D, bytes_accessed=4 << 20, transcendentals=0),
    )(state, keep, from_sib, from_far)
    sources = [*relayed, *back]
    kept = [(rows, D)] * len(relayed) + [(slots, D)]
    final = pl.pallas_call(
        functools.partial(combine_kernel, len(sources), len(back)),
        out_shape=shape(rows, D),
        in_specs=[VMEM] * 3 + [ANY] * len(sources),
        out_specs=HBM,
        scratch_shapes=[pltpu.VMEM(dims, BF16) for dims in kept]
        + [pltpu.VMEM((rows, D), BF16), pltpu.SemaphoreType.DMA((2, 16))],
        compiler_params=pltpu.CompilerParams(vmem_limit_bytes=56 << 20),
        cost_estimate=pl.CostEstimate(flops=0, bytes_accessed=0, transcendentals=0),
    )(high, low, blend, *sources)

    pair_row = grp // 4 * 2 + grp % 2
    flags = jnp.sum(
        jnp.where((jnp.arange(migrate.shape[0], dtype=jnp.int32) == pair_row)[:, None], migrate, 0), axis=0
    )
    page_moved = jnp.repeat(flags, PG) == 1
    suffix_cache = jnp.where(page_moved[:, None], partner, own_cache)
    return (final[None], suffix_cache[None])


def solution(mesh):
    placed = (
        P("grp", "req", None),
        P("grp", "req", None),
        P("grp", "req", None),
        P("grp", "req", None),
        P("grp", "req", None),
        P(("req", "grp"), None),
        P(),
        P("grp", "req", None),
        P("grp", "req", None),
        P("grp", None),
        P(None, "req"),
        P("req", None, "grp"),
        P("req", None, "grp"),
        P("req", "grp", None),
        P(None, "grp"),
        P(None, "grp"),
        P("grp", None),
        P(),
    )
    return jax.shard_map(
        local,
        mesh=mesh,
        in_specs=placed,
        out_specs=(P("grp", "req", None), P("grp", "req", None)),
        check_vma=False,
    )
```
